32 devices in a mesh: sub: 8 (over z, x), col: 4 (over y, core).
Axes of the slice: x: 2, y: 2, z: 4, core: 2. Of those that a mesh axis runs over, the one named last changes fastest.
Arguments:
- trace_start: bfloat16 [8, 4, 1536, 128], P('sub', 'col'), may hold values from -6 to 6
- neumann_load: bfloat16 [8, 4, 1536, 128], P('sub', 'col'), may hold values from -6 to 6
- double_layer: bfloat16 [8, 4, 1536, 1536], P('sub', 'col'), may hold values from -0.15625 to 0.15625
- single_inverse: bfloat16 [8, 4, 1536, 1536], P('sub', 'col'), may hold values from -0.15625 to 0.15625
- interface_nodes: int32 [8, 4, 8, 128], P('sub', 'col'), may hold values from -1 to 1023, as said below
- node_mode: int32 [8, 4, 1536], P('sub', 'col'), may hold values from 0 to 63
- mode_weight: bfloat16 [8, 4, 1536], P('sub', 'col'), may hold values from 0.5 to 1.5
- coarse_inverse: bfloat16 [2048, 2048], P('sub', 'col'), may hold values from -0.015625 to 0.015625
Outputs:
- final_trace: bfloat16 [8, 4, 1536, 128], P('sub', 'col')
- final_residual: bfloat16 [8, 4, 1536, 128], P('sub', 'col')
The draws below stay inside these ranges and needn't reach their ends.
Inputs may be any that keep to these rules, and one draw needn't show every extreme that they name: `interface_nodes`: entry k of block (s, d) is a boundary node of s, within nodes d * 128 to (d + 1) * 128 - 1, distinct within the block, and matches entry k of the neighbour's block for direction 7 - d; valid entries come first and the rest are -1; blocks toward outside the grid are all -1; blocks of directions 1, 3, 4, 6 have 128 / 2 to 128 valid entries, the others 1 to 16, and some block has 128.
All inputs are finite; a program needn't handle non-finite values.
Results may differ from the reference program's by a relative error of at most 0.019.
Values may be sent and summed in bfloat16 or wider, within the bound.
No kernel may reach another device: no remote copies, remote signals or barrier semaphores. Data moves between devices by JAX's collectives and lax.ppermute only.
A program may use at most 64 MiB of HBM per device.

```python
import jax
import jax.numpy as jnp
import numpy as np
from jax import lax

M = 1536
R = 128
MODES = 64
IFACE = 128
ITERS = 3
GX = 8
GY = 4
NC = 2048


DIRECTIONS = ((-1, -1), (-1, 0), (-1, 1), (0, -1), (0, 1), (1, -1), (1, 0), (1, 1))


def draw_interface_nodes(key, part):
    face_len = jax.random.randint(jax.random.fold_in(key, 11), (GX, GY, 8), IFACE // 2, IFACE + 1)
    corner_len = jax.random.randint(jax.random.fold_in(key, 37), (GX, GY, 8), 1, IFACE // 8 + 1)
    corner_table = np.array([abs(pair[0]) + abs(pair[1]) == 2 for pair in DIRECTIONS])
    edge_len = jnp.where(jnp.asarray(corner_table)[None, None, :], corner_len, face_len)
    edge_len = edge_len.at[0, 0, 4].set(IFACE)
    row_index = jnp.arange(GX)[:, None]
    col_index = jnp.arange(GY)[None, :]
    lengths = []
    for toward in range(8):
        row_step, col_step = DIRECTIONS[toward]
        inside = (row_index + row_step >= 0) & (row_index + row_step < GX) & (col_index + col_step >= 0) & (col_index + col_step < GY)
        if toward >= 4:
            owner_len = edge_len[:, :, toward]
        else:
            owner_len = jnp.roll(edge_len[:, :, 7 - toward], (-row_step, -col_step), axis=(0, 1))
        lengths.append(jnp.where(inside, owner_len, 0))
    length_all = jnp.stack(lengths, axis=2)
    shuffled = jax.random.permutation(jax.random.fold_in(key, 23), jnp.broadcast_to(jnp.arange(IFACE, dtype=jnp.int32), (GX, GY, 8, IFACE)), axis=-1, independent=True)
    node_ids = jnp.arange(8, dtype=jnp.int32)[:, None] * IFACE + shuffled
    position = jnp.arange(IFACE, dtype=jnp.int32)
    return jnp.where(position < length_all[..., None], node_ids, -1).astype(jnp.int32)


def set_ends(result, rng, low, largest):
    shape = result.shape
    place = [jax.random.randint(jax.random.fold_in(rng, axis), (), 0, shape[axis]) for axis in range(len(shape))]
    result = result.at[tuple(place)].set(low)
    longest = shape.index(max(shape))
    place[longest] = (place[longest] + 1) % shape[longest]
    return result.at[tuple(place)].set(largest)


def block_levels(own_key, extent, cuts, low, high):
    def one(dim, blocks):
        draws = jax.random.uniform(jax.random.fold_in(jax.random.fold_in(own_key, 6), dim), (blocks,), jnp.float32, low / len(cuts), high / len(cuts))
        return jnp.repeat(jnp.exp(draws), extent[dim] // blocks).reshape((-1,) + (1,) * (len(extent) - dim - 1))

    factor_of = one(*cuts[0])
    for cut in cuts[1:]:
        factor_of = factor_of * one(*cut)
    return factor_of


def centred(own_key, shape, scale, most, pieces=(), kind=jnp.bfloat16):
    loudness = block_levels(own_key, shape, pieces, -0.22, 0.18) if pieces else 1.0
    values = jax.random.normal(own_key, shape, jnp.float32) * scale * loudness
    return jnp.minimum(jnp.maximum(values, -most), most).astype(kind)


def setup_inputs(seed: int = 0) -> dict:
    streams_of = jax.random.split(jax.random.key(seed), 9)
    return {
        "trace_start": centred(streams_of[0], (GX, GY, M, R), 1.0, 6.0, ((0, 8), (1, 4))),
        "neumann_load": centred(streams_of[1], (GX, GY, M, R), 1.0, 6.0, ((0, 8), (1, 4))),
        "double_layer": centred(streams_of[2], (GX, GY, M, M), M ** -0.5, 0.15625, ((0, 8), (1, 4))),
        "single_inverse": centred(streams_of[3], (GX, GY, M, M), M ** -0.5, 0.15625, ((0, 8), (1, 4))),
        "interface_nodes": draw_interface_nodes(jax.random.fold_in(streams_of[8], 71), 0),
        "node_mode": set_ends(jax.random.randint(streams_of[5], (GX, GY, M), 0, MODES), jax.random.fold_in(streams_of[5], 1), 0, MODES - 1).astype(jnp.int32),
        "mode_weight": jnp.clip(0.5 + 1.0 * jax.random.uniform(streams_of[6], (GX, GY, M), jnp.float32) ** block_levels(streams_of[6], (GX, GY, M), ((0, 8), (1, 4)), -0.2, 0.2), 0.5, 1.5).astype(jnp.bfloat16),
        "coarse_inverse": centred(streams_of[7], (NC, NC), ((64 * NC) ** -0.5), 0.015625, ((0, 8), (1, 4))),
    }


DIRECTIONS = ((-1, -1), (-1, 0), (-1, 1), (0, -1), (0, 1), (1, -1), (1, 0), (1, 1))


def steklov(items):
    kernel, inverse, trace_now = items
    mixed_trace = (0.5 * trace_now.astype(jnp.float32) + jnp.dot(kernel, trace_now, preferred_element_type=jnp.float32)).astype(jnp.bfloat16)
    return jnp.dot(inverse, mixed_trace, preferred_element_type=jnp.float32).astype(jnp.bfloat16)


def pick_rows(values, indices):
    return values[indices]


def add_rows(values, indices):
    holder = jnp.zeros((M + 1, R), jnp.float32)
    return holder.at[indices].add(values.astype(jnp.float32))[:M]


def reference(trace_start, neumann_load, double_layer, single_inverse, interface_nodes, node_mode, mode_weight, coarse_inverse):
    flat_kernel = double_layer.reshape(GX * GY, M, M)
    flat_inverse = single_inverse.reshape(GX * GY, M, M)
    valid = (interface_nodes >= 0).reshape(GX, GY, 8 * IFACE)
    safe_index = jnp.where(valid, interface_nodes.reshape(GX, GY, 8 * IFACE), 0).astype(jnp.int32)
    target_index = jnp.where(valid, interface_nodes.reshape(GX, GY, 8 * IFACE), M).astype(jnp.int32)
    mode_range = jnp.arange(MODES, dtype=jnp.int32)
    mode_basis = jnp.where(node_mode[:, :, None, :] == mode_range[None, None, :, None], mode_weight[:, :, None, :], jnp.zeros((), jnp.bfloat16))
    basis_wide = mode_basis.astype(jnp.float32)
    trace_now = trace_start
    residual = trace_start
    for iteration in range(ITERS):
        flux_now = lax.map(steklov, (flat_kernel, flat_inverse, trace_now.reshape(GX * GY, M, R))).reshape(GX, GY, M, R)
        picked = jax.vmap(jax.vmap(pick_rows))(flux_now, safe_index)
        outgoing = jnp.where(valid[..., None], picked, jnp.zeros((), jnp.bfloat16)).reshape(GX, GY, 8, IFACE, R)
        arrivals = []
        for toward in range(8):
            row_step, col_step = DIRECTIONS[toward]
            source = jnp.pad(outgoing[:, :, 7 - toward], ((1, 1), (1, 1), (0, 0), (0, 0)))
            arrivals.append(source[1 + row_step:1 + row_step + GX, 1 + col_step:1 + col_step + GY])
        received = jnp.stack(arrivals, axis=2).reshape(GX, GY, 8 * IFACE, R)
        assembled = flux_now.astype(jnp.float32) + jax.vmap(jax.vmap(add_rows))(received, target_index)
        residual = (neumann_load.astype(jnp.float32) - assembled).astype(jnp.bfloat16)
        residual = lax.optimization_barrier(residual)
        coarse_rhs = jnp.einsum("abmn,abnr->abmr", basis_wide, residual.astype(jnp.float32), precision=lax.Precision.HIGHEST).astype(jnp.bfloat16)
        column_vector = jnp.transpose(coarse_rhs, (1, 0, 2, 3)).reshape(NC, R)
        coarse_out = jnp.dot(coarse_inverse, column_vector, preferred_element_type=jnp.float32).astype(jnp.bfloat16).reshape(GX, GY, MODES, R)
        coarse_out = lax.optimization_barrier(coarse_out)
        correction = jnp.einsum("abmn,abmr->abnr", basis_wide, coarse_out.astype(jnp.float32), precision=lax.Precision.HIGHEST)
        trace_now = (trace_now.astype(jnp.float32) + 0.25 * residual.astype(jnp.float32) + correction).astype(jnp.bfloat16)
    return trace_now, residual
```

```python
import jax
import jax.numpy as jnp
from jax import lax
from jax.sharding import PartitionSpec as P

MODES = 64
ITERS = 3

bf16 = jnp.bfloat16
f32 = jnp.float32


def dot(a, b, dims=(((1,), (0,)), ((), ()))):
    return lax.dot_general(a, b, dims, preferred_element_type=f32)


def pair_relay(axis, forward, backward):
    devices = lax.axis_size(axis)
    even = lax.axis_index(axis) % 2 == 0
    sent = jnp.stack([jnp.where(even, forward, backward), jnp.where(even, backward, forward)])
    got = lax.ppermute(sent, axis, [(i, i ^ 1) for i in range(devices)])
    onward = [(i, i + 2) for i in range(0, devices - 2, 2)]
    back = [(i + 2, i) for i in range(1, devices - 2, 2)]
    relayed = lax.ppermute(got[1], axis, onward + back)
    from_next = jnp.where(even, got[0], relayed)
    from_previous = jnp.where(even, relayed, got[0])
    return from_next, from_previous


def exchange(outgoing, corner):
    face = outgoing.shape[1]
    right = jnp.concatenate([outgoing[4], outgoing[2, :corner], outgoing[7, :corner]])
    left = jnp.concatenate([outgoing[3], outgoing[0, :corner], outgoing[5, :corner]])
    from_right, from_left = pair_relay("col", right, left)
    up = jnp.concatenate([outgoing[6], from_right[face + corner :], from_left[face + corner :]])
    down = jnp.concatenate(
        [outgoing[1], from_right[face : face + corner], from_left[face : face + corner]]
    )
    from_up, from_down = pair_relay("sub", up, down)
    wide = lambda rows: jnp.pad(rows, ((0, face - corner), (0, 0)))
    return jnp.stack(
        [
            wide(from_down[face + corner :]),
            from_down[:face],
            wide(from_down[face : face + corner]),
            from_left[:face],
            from_right[:face],
            wide(from_up[face + corner :]),
            from_up[:face],
            wide(from_up[face : face + corner]),
        ]
    )


def sum_over_columns(partial, axis):
    devices = lax.axis_size(axis)
    index = lax.axis_index(axis)
    step = devices // 2
    while step:
        half = partial.shape[0] // 2
        upper = (index // step) % 2 == 1
        low, high = partial[:half], partial[half:]
        sent = jnp.where(upper, low, high).astype(bf16)
        got = lax.ppermute(sent, axis, [(i, i ^ step) for i in range(devices)])
        partial = jnp.where(upper, high, low) + got.astype(f32)
        step //= 2
    return partial.astype(bf16)


def local(
    trace_start,
    neumann_load,
    double_layer,
    single_inverse,
    interface_nodes,
    node_mode,
    mode_weight,
    coarse_inverse,
):
    trace_now = trace_start[0, 0]
    load_block = neumann_load[0, 0].astype(f32)
    kernel = double_layer[0, 0]
    inverse = single_inverse[0, 0]
    node_count, rhs_count = trace_now.shape
    interface = interface_nodes[0, 0]
    slot_count = interface.shape[1]
    corner = slot_count // 8
    band_rows = 8 * slot_count
    local_index = interface - (jnp.arange(8, dtype=jnp.int32) * slot_count)[:, None]
    selector = (
        local_index[:, :, None] == jnp.arange(slot_count, dtype=jnp.int32)[None, None, :]
    ).astype(bf16)
    mode_basis = jnp.where(
        node_mode[0, 0][None, :] == jnp.arange(MODES, dtype=jnp.int32)[:, None],
        mode_weight[0, 0][None, :],
        jnp.zeros((), bf16),
    )
    residual = trace_now
    rest_zeros = jnp.zeros((node_count - band_rows, rhs_count), f32)
    subs = lax.axis_size("sub")
    for iteration in range(ITERS):
        mixed = (0.5 * trace_now.astype(f32) + dot(kernel, trace_now)).astype(bf16)
        flux_now = dot(inverse, mixed).astype(bf16)
        banded = flux_now[:band_rows].reshape(8, slot_count, rhs_count)
        outgoing = jnp.einsum(
            "dpq,dqr->dpr", selector, banded, preferred_element_type=f32
        ).astype(bf16)
        received = exchange(outgoing, corner)
        placed = jnp.einsum("dpq,dpr->dqr", selector, received, preferred_element_type=f32)
        placed = placed.reshape(band_rows, rhs_count)
        assembled = flux_now.astype(f32) + jnp.concatenate([placed, rest_zeros], axis=0)
        residual = (load_block - assembled).astype(bf16)
        coarse_rhs = dot(mode_basis, residual).astype(bf16)
        copies = jnp.broadcast_to(coarse_rhs[None], (subs, MODES, rhs_count))
        gathered = lax.all_to_all(copies.reshape(subs * MODES, rhs_count), "sub", 0, 0, tiled=True)
        coarse_out = sum_over_columns(dot(coarse_inverse, gathered), "col")
        correction = dot(mode_basis, coarse_out, (((0,), (0,)), ((), ())))
        trace_now = (
            trace_now.astype(f32) + 0.25 * residual.astype(f32) + correction
        ).astype(bf16)
    return (trace_now[None, None], residual[None, None])


def solution(mesh):
    placed = (
        P("sub", "col", None, None),
        P("sub", "col", None, None),
        P("sub", "col", None, None),
        P("sub", "col", None, None),
        P("sub", "col", None, None),
        P("sub", "col", None),
        P("sub", "col", None),
        P("sub", "col"),
    )
    return jax.shard_map(
        local,
        mesh=mesh,
        in_specs=placed,
        out_specs=(P("sub", "col", None, None), P("sub", "col", None, None)),
        check_vma=False,
    )
```

```python
import functools

import jax
import jax.numpy as jnp
from jax import lax
from jax.experimental import pallas as pl
from jax.experimental.pallas import tpu as pltpu
from jax.sharding import PartitionSpec as P

MODES = 64
ITERS = 3

bf16 = jnp.bfloat16
f32 = jnp.float32


def dot(a, b, dims=(((1,), (0,)), ((), ()))):
    return lax.dot_general(a, b, dims, preferred_element_type=f32)


def products_kernel(face, corner, chunk, u_ref, k_hbm, s_hbm, sel_ref, flux_ref, packed_ref, kbuf, sbuf, mixed, sems):
    nodes = u_ref.shape[0]
    count = nodes // chunk
    copies = []
    for which, (source, target) in enumerate(((k_hbm, kbuf), (s_hbm, sbuf))):
        for i in range(count):
            rows = pl.ds(i * chunk, chunk)
            copy = pltpu.make_async_copy(source.at[rows], target.at[rows], sems.at[which, i])
            copy.start()
            copies.append(copy)
    u = u_ref[...]
    for i in range(count):
        rows = pl.ds(i * chunk, chunk)
        copies[i].wait()
        product = dot(kbuf[rows, :], u)
        mixed[rows, :] = (0.5 * u_ref[rows, :].astype(f32) + product).astype(bf16)
    m = mixed[...]
    for i in range(count):
        rows = pl.ds(i * chunk, chunk)
        copies[count + i].wait()
        flux_ref[rows, :] = dot(sbuf[rows, :], m).astype(bf16)
    at = 0
    for d, size in ((4, face), (2, corner), (7, corner), (3, face), (0, corner), (5, corner), (6, face), (1, face)):
        picked = dot(sel_ref[d, :size, :], flux_ref[d * face : (d + 1) * face, :])
        packed_ref[at : at + size, :] = picked.astype(bf16)
        at += size


def products(u, kernel, inverse, selector):
    nodes, width = u.shape
    face = selector.shape[1]
    corner = face // 8
    chunk = 256 if nodes % 256 == 0 else nodes
    vmem = pl.BlockSpec(memory_space=pltpu.VMEM)
    hbm = pl.BlockSpec(memory_space=pl.ANY)
    return pl.pallas_call(
        functools.partial(products_kernel, face, corner, chunk),
        out_shape=(
            jax.ShapeDtypeStruct((nodes, width), bf16),
            jax.ShapeDtypeStruct((4 * (face + corner), width), bf16),
        ),
        in_specs=[vmem, hbm, hbm, vmem],
        out_specs=(vmem, vmem),
        scratch_shapes=[
            pltpu.VMEM((nodes, nodes), bf16),
            pltpu.VMEM((nodes, nodes), bf16),
            pltpu.VMEM((nodes, width), bf16),
            pltpu.SemaphoreType.DMA((2, nodes // chunk)),
        ],
        compiler_params=pltpu.CompilerParams(vmem_limit_bytes=32 * 1024 * 1024),
        cost_estimate=pl.CostEstimate(
            flops=4 * nodes * nodes * width, bytes_accessed=4 * nodes * nodes, transcendentals=0
        ),
        name="products",
    )(u, kernel, inverse, selector)


def pair_relay(axis, forward, backward):
    devices = lax.axis_size(axis)
    even = lax.axis_index(axis) % 2 == 0
    sent = jnp.stack([jnp.where(even, forward, backward), jnp.where(even, backward, forward)])
    got = lax.ppermute(sent, axis, [(i, i ^ 1) for i in range(devices)])
    onward = [(i, i + 2) for i in range(0, devices - 2, 2)]
    back = [(i + 2, i) for i in range(1, devices - 2, 2)]
    relayed = lax.ppermute(got[1], axis, onward + back)
    from_next = jnp.where(even, got[0], relayed)
    from_previous = jnp.where(even, relayed, got[0])
    return from_next, from_previous


def exchange(packed, face, corner):
    group = face + 2 * corner
    right, left = packed[:group], packed[group : 2 * group]
    six, one = packed[2 * group : 2 * group + face], packed[2 * group + face :]
    from_right, from_left = pair_relay("col", right, left)
    up = jnp.concatenate([six, from_right[face + corner :], from_left[face + corner :]])
    down = jnp.concatenate(
        [one, from_right[face : face + corner], from_left[face : face + corner]]
    )
    from_up, from_down = pair_relay("sub", up, down)
    wide = lambda rows: jnp.pad(rows, ((0, face - corner), (0, 0)))
    return jnp.stack(
        [
            wide(from_down[face + corner :]),
            from_down[:face],
            wide(from_down[face : face + corner]),
            from_left[:face],
            from_right[:face],
            wide(from_up[face + corner :]),
            from_up[:face],
            wide(from_up[face : face + corner]),
        ]
    )


def sum_over_columns(partial, axis):
    devices = lax.axis_size(axis)
    index = lax.axis_index(axis)
    step = devices // 2
    while step:
        half = partial.shape[0] // 2
        upper = (index // step) % 2 == 1
        low, high = partial[:half], partial[half:]
        sent = jnp.where(upper, low, high).astype(bf16)
        got = lax.ppermute(sent, axis, [(i, i ^ step) for i in range(devices)])
        partial = jnp.where(upper, high, low) + got.astype(f32)
        step //= 2
    return partial.astype(bf16)


def local(
    trace_start,
    neumann_load,
    double_layer,
    single_inverse,
    interface_nodes,
    node_mode,
    mode_weight,
    coarse_inverse,
):
    trace_now = trace_start[0, 0]
    load_block = neumann_load[0, 0].astype(f32)
    kernel = double_layer[0, 0]
    inverse = single_inverse[0, 0]
    node_count, rhs_count = trace_now.shape
    interface = interface_nodes[0, 0]
    slot_count = interface.shape[1]
    corner = slot_count // 8
    band_rows = 8 * slot_count
    local_index = interface - (jnp.arange(8, dtype=jnp.int32) * slot_count)[:, None]
    selector = (
        local_index[:, :, None] == jnp.arange(slot_count, dtype=jnp.int32)[None, None, :]
    ).astype(bf16)
    mode_basis = jnp.where(
        node_mode[0, 0][None, :] == jnp.arange(MODES, dtype=jnp.int32)[:, None],
        mode_weight[0, 0][None, :],
        jnp.zeros((), bf16),
    )
    residual = trace_now
    rest_zeros = jnp.zeros((node_count - band_rows, rhs_count), f32)
    subs = lax.axis_size("sub")
    for iteration in range(ITERS):
        flux_now, packed = products(trace_now, kernel, inverse, selector)
        received = exchange(packed, slot_count, corner)
        placed = jnp.einsum("dpq,dpr->dqr", selector, received, preferred_element_type=f32)
        placed = placed.reshape(band_rows, rhs_count)
        assembled = flux_now.astype(f32) + jnp.concatenate([placed, rest_zeros], axis=0)
        residual = (load_block - assembled).astype(bf16)
        coarse_rhs = dot(mode_basis, residual).astype(bf16)
        copies = jnp.broadcast_to(coarse_rhs[None], (subs, MODES, rhs_count))
        gathered = lax.all_to_all(copies.reshape(subs * MODES, rhs_count), "sub", 0, 0, tiled=True)
        coarse_out = sum_over_columns(dot(coarse_inverse, gathered), "col")
        correction = dot(mode_basis, coarse_out, (((0,), (0,)), ((), ())))
        trace_now = (
            trace_now.astype(f32) + 0.25 * residual.astype(f32) + correction
        ).astype(bf16)
    return (trace_now[None, None], residual[None, None])


def solution(mesh):
    placed = (
        P("sub", "col", None, None),
        P("sub", "col", None, None),
        P("sub", "col", None, None),
        P("sub", "col", None, None),
        P("sub", "col", None, None),
        P("sub", "col", None),
        P("sub", "col", None),
        P("sub", "col"),
    )
    return jax.shard_map(
        local,
        mesh=mesh,
        in_specs=placed,
        out_specs=(P("sub", "col", None, None), P("sub", "col", None, None)),
        check_vma=False,
    )
```

```python
import functools

import jax
import jax.numpy as jnp
from jax import lax
from jax.experimental import pallas as pl
from jax.experimental.pallas import tpu as pltpu
from jax.sharding import PartitionSpec as P

MODES = 64
ITERS = 3
LANES = 128

bf16 = jnp.bfloat16
f32 = jnp.float32
BOTH = ("sub", "col")
DIRECTIONS = ((-1, -1), (-1, 0), (-1, 1), (0, -1), (0, 1), (1, -1), (1, 0), (1, 1))
PACKED = ((4, 1), (2, 0), (7, 0), (3, 1), (0, 0), (5, 0), (6, 1), (1, 1))

vmem = pl.BlockSpec(memory_space=pltpu.VMEM)
smem = pl.BlockSpec(memory_space=pltpu.SMEM)
hbm = pl.BlockSpec(memory_space=pl.ANY)
shape_of = jax.ShapeDtypeStruct
params = pltpu.CompilerParams(vmem_limit_bytes=24 * 1024 * 1024)
large = pltpu.CompilerParams(vmem_limit_bytes=50 * 1024 * 1024)


def dot(a, b):
    return jnp.dot(a, b, preferred_element_type=f32)


def pick(face, sel_ref, flux_ref, packed_ref):
    at = 0
    for d, whole in PACKED:
        size = face if whole else face // 8
        rows = dot(sel_ref[d, :size, :], flux_ref[d * face : (d + 1) * face, :])
        packed_ref[at : at + size, :] = rows.astype(bf16)
        at += size


def load_kernel(face, chunk, ahead, u_ref, k_hbm, s_hbm, sel_ref, flux_ref, packed_ref, k_ref, s_ref, mixed, sems):
    count = u_ref.shape[0] // chunk
    copies = []
    for which, (source, target) in enumerate(((k_hbm, k_ref), (s_hbm, s_ref))):
        for i in range(count):
            rows = pl.ds(i * chunk, chunk)
            copies.append(pltpu.make_async_copy(source.at[rows], target.at[rows], sems.at[which, i]))
    for copy in copies[:ahead]:
        copy.start()
    u = u_ref[...]
    for i in range(2 * count):
        copies[i].wait()
        if i + ahead < 2 * count:
            copies[i + ahead].start()
        rows = pl.ds(i % count * chunk, chunk)
        if i < count:
            mixed[rows, :] = (0.5 * u_ref[rows, :].astype(f32) + dot(k_ref[rows, :], u)).astype(bf16)
        else:
            flux_ref[rows, :] = dot(s_ref[rows, :], mixed[...]).astype(bf16)
    pick(face, sel_ref, flux_ref, packed_ref)


def products_kernel(face, chunk, u_ref, k_ref, s_ref, sel_ref, flux_ref, packed_ref, mixed):
    u = u_ref[...]
    for i in range(u_ref.shape[0] // chunk):
        rows = pl.ds(i * chunk, chunk)
        mixed[rows, :] = (0.5 * u_ref[rows, :].astype(f32) + dot(k_ref[rows, :], u)).astype(bf16)
    m = mixed[...]
    for i in range(u_ref.shape[0] // chunk):
        rows = pl.ds(i * chunk, chunk)
        flux_ref[rows, :] = dot(s_ref[rows, :], m).astype(bf16)
    pick(face, sel_ref, flux_ref, packed_ref)


def products(u, kernel, inverse, selector, load=False):
    nodes, width = u.shape
    face = selector.shape[1]
    chunk = 256 if nodes % 256 == 0 else nodes
    outs = [shape_of((nodes, width), bf16), shape_of((4 * (face + face // 8), width), bf16)]
    scratch = [pltpu.VMEM((nodes, width), bf16)]
    body = functools.partial(products_kernel, face, chunk)
    if load:
        outs += [pltpu.VMEM((nodes, nodes), bf16)] * 2
        scratch += [pltpu.SemaphoreType.DMA((2, nodes // chunk))]
        body = functools.partial(load_kernel, face, chunk, 3)
    return pl.pallas_call(
        body,
        out_shape=outs,
        in_specs=[vmem] + [hbm if load else vmem] * 2 + [vmem],
        out_specs=[vmem] * len(outs),
        scratch_shapes=scratch,
        compiler_params=large if load else params,
        cost_estimate=pl.CostEstimate(
            flops=4 * nodes * nodes * 2 * LANES, bytes_accessed=4 * nodes * nodes, transcendentals=0
        ),
        name="load_products" if load else "products",
    )(u, kernel, inverse, selector)


def update_kernel(face, first, place, rows_ref, flux_ref, load_ref, state_ref, selt_ref, basis_ref, tall_ref, c_ref, w_ref, wrows_ref, res_ref, next_ref, u_ref, rhs_ref):
    corner = face // 8
    modes = basis_ref.shape[0]
    found = {4: (0, 0), 3: (1, 0), 6: (2, 0), 1: (3, 0)}
    found |= {7: (2, face), 5: (2, face + corner), 2: (3, face), 0: (3, face + corner)}
    flux = flux_ref[...].astype(f32)
    state = state_ref[...].astype(f32)
    if not first:
        start = pl.multiple_of(place[1], modes)
        own = c_ref[place[0], pl.ds(start, modes), :]
        flux = (flux + dot(w_ref[:, :modes], own)).astype(bf16).astype(f32)
        state = state + dot(tall_ref[:, :modes], own)
    assembled = []
    for d in range(8):
        group, at = found[d]
        size = face if DIRECTIONS[d][0] * DIRECTIONS[d][1] == 0 else corner
        arrived = rows_ref[group, at : at + size, :]
        if not first:
            start = pl.multiple_of(place[2 * d + 3], modes)
            theirs = c_ref[place[2 * d + 2], pl.ds(start, modes), :]
            wide = wrows_ref[group, at : at + size, :modes]
            arrived = (arrived.astype(f32) + dot(wide, theirs)).astype(bf16)
        assembled.append(flux[d * face : (d + 1) * face] + dot(selt_ref[d, :, :size], arrived))
    assembled.append(flux[8 * face :])
    residual = (load_ref[...].astype(f32) - jnp.concatenate(assembled)).astype(bf16)
    res_ref[...] = residual
    following = state + 0.25 * residual.astype(f32)
    next_ref[...] = following
    u_ref[...] = following.astype(bf16)
    rhs_ref[...] = dot(basis_ref[...], residual).astype(bf16)


def update(place, rows, flux, load, state, selector_t, basis, tall, coarse, wide, wide_rows):
    first = coarse is None
    nodes, width = load.shape
    modes = basis.shape[0]
    operands = [place, rows, flux, load, state, selector_t, basis, tall]
    body = functools.partial(update_kernel, selector_t.shape[1], first)
    if first:
        inner = body
        body = lambda *refs: inner(*refs[:8], None, None, None, *refs[8:])
    else:
        operands += [coarse, wide, wide_rows]
    return pl.pallas_call(
        body,
        out_shape=[
            shape_of((nodes, width), bf16),
            shape_of((nodes, width), f32),
            shape_of((nodes, width), bf16),
            shape_of((modes, width), bf16),
        ],
        in_specs=[smem] + [vmem] * (len(operands) - 1),
        out_specs=[vmem] * 4,
        compiler_params=params,
        cost_estimate=pl.CostEstimate(
            flops=8 * nodes * LANES * width, bytes_accessed=12 * nodes * width, transcendentals=0
        ),
        name="update",
    )(*operands)


def coarse_kernel(modes, place, pieces_ref, *refs):
    matrices, out_ref, full = refs[:-2], refs[-2], refs[-1]
    count = pieces_ref.shape[0]
    for m in range(count):
        start = pl.multiple_of((place[0] ^ m) * modes, modes)
        for j in range(2):
            full[j, pl.ds(start, modes), :] = pieces_ref[m, j * modes : (j + 1) * modes, :]
    for i, matrix in enumerate(matrices):
        out_ref[i] = dot(matrix[0], full[0]) + dot(matrix[1], full[1])


def coarse_product(place, pieces, matrices):
    count, twice, width = pieces.shape
    rows = matrices[0].shape[1]
    return pl.pallas_call(
        functools.partial(coarse_kernel, twice // 2),
        out_shape=shape_of((len(matrices), rows, width), f32),
        in_specs=[smem] + [vmem] * (1 + len(matrices)),
        out_specs=vmem,
        scratch_shapes=[pltpu.VMEM((2, count * twice // 2, width), bf16)],
        compiler_params=params,
        cost_estimate=pl.CostEstimate(
            flops=2 * len(matrices) * rows * count * twice * width,
            bytes_accessed=2 * len(matrices) * rows * count * twice,
            transcendentals=0,
        ),
        name="coarse_product",
    )(place, pieces, *matrices)


def chip_pairs(subs, cols, step):
    pairs = []
    for sub in range(subs):
        for chip in range(cols // 2):
            to = step(sub, chip)
            if 0 <= to[0] < subs and 0 <= to[1] < cols // 2:
                pairs.append((sub * cols + 2 * chip + 1, to[0] * cols + 2 * to[1] + 1))
    return pairs


class Moves:
    def __init__(self):
        self.subs, self.cols = lax.axis_size("sub"), lax.axis_size("col")
        self.even_sub = lax.axis_index("sub") % 2 == 0
        self.odd_core = lax.axis_index("col") % 2 == 1
        self.chip = lax.axis_index("col") // 2

    def between(self, value, step):
        return lax.ppermute(value, BOTH, chip_pairs(self.subs, self.cols, step))

    def to_odd(self, value):
        return lax.ppermute(value, "col", [(i, i + 1) for i in range(0, self.cols, 2)])

    def to_even(self, value):
        return lax.ppermute(value, "col", [(i + 1, i) for i in range(0, self.cols, 2)])

    def pair(self, value):
        return self.between(value, lambda sub, chip: (sub ^ 1, chip))

    def relay(self, value):
        return self.between(value, lambda sub, chip: (sub + 2 if sub % 2 == 0 else sub - 2, chip))

    def sum_chips(self, value):
        bit = 1
        while bit < self.cols // 2:
            got = self.between(value.astype(bf16), lambda sub, chip: (sub, chip ^ bit))
            value = value + got.astype(f32)
            bit *= 2
        value = value.astype(bf16)
        return jnp.where(self.odd_core, value, self.to_even(value))

    def gather_rows(self, value):
        pieces = value[None]
        while pieces.shape[0] < self.subs:
            bit = pieces.shape[0]
            got = self.between(pieces, lambda sub, chip: (sub ^ bit, chip))
            pieces = jnp.concatenate([pieces, got])
        return pieces

    def exchange(self, packed, face):
        corner = face // 8
        group = face + 2 * corner
        right_way, left_way = slice(0, group), slice(group, 2 * group)
        even = self.to_odd(packed)
        if self.cols == 4:
            sent = jnp.where(self.chip == 0, packed[right_way], even[left_way])
            from_right = from_left = self.between(sent, lambda sub, chip: (sub, 1 - chip))
        else:
            from_left = self.between(packed[right_way], lambda sub, chip: (sub, chip + 1))
            from_right = self.between(even[left_way], lambda sub, chip: (sub, chip - 1))
        right = (packed[left_way], from_right)
        left = (from_left, even[right_way])
        up, down = [], []
        for j, mine in enumerate((even, packed)):
            six, one = mine[2 * group : 2 * group + face], mine[2 * group + face :]
            up.append(jnp.concatenate([six, right[j][face + corner :], left[j][face + corner :]]))
            down.append(
                jnp.concatenate([one, right[j][face : face + corner], left[j][face : face + corner]])
            )
        up, down = jnp.stack(up), jnp.stack(down)
        got = self.pair(
            jnp.stack([jnp.where(self.even_sub, up, down), jnp.where(self.even_sub, down, up)])
        )
        relayed = self.relay(got[1])
        above = jnp.where(self.even_sub, got[0], relayed)
        below = jnp.where(self.even_sub, relayed, got[0])
        theirs, own = (jnp.stack([right[j], left[j], above[j], below[j]]) for j in range(2))
        return jnp.where(self.odd_core, own, self.to_even(theirs))


def local(
    trace_start,
    neumann_load,
    double_layer,
    single_inverse,
    interface_nodes,
    node_mode,
    mode_weight,
    coarse_inverse,
):
    moves = Moves()
    subs, cols = moves.subs, moves.cols
    row, col = lax.axis_index("sub"), lax.axis_index("col")
    trace = trace_start[0, 0]
    load = neumann_load[0, 0]
    width = trace.shape[1]
    interface = interface_nodes[0, 0]
    face = interface.shape[1]
    position = interface - (jnp.arange(8, dtype=jnp.int32) * face)[:, None]
    slots = jnp.arange(face, dtype=jnp.int32)
    selector = (position[:, :, None] == slots[None, None, :]).astype(bf16)
    selector_t = (position[:, None, :] == slots[None, :, None]).astype(bf16)
    nothing = jnp.zeros((), bf16)
    mode, weight = node_mode[0, 0], mode_weight[0, 0]
    modes = jnp.arange(MODES, dtype=jnp.int32)
    lanes = jnp.arange(LANES, dtype=jnp.int32)
    basis = jnp.where(mode[None, :] == modes[:, None], weight[None, :], nothing)
    tall = jnp.where(mode[:, None] == lanes[None, :], weight[:, None], nothing)

    place = [jnp.zeros((), jnp.int32), col * MODES]
    for row_step, col_step in DIRECTIONS:
        source = {0: 0, 1: jnp.where(moves.even_sub, 1, 2), -1: jnp.where(moves.even_sub, 2, 1)}
        place += [source[row_step], jnp.clip(col + col_step, 0, cols - 1) * MODES]
    place = jnp.stack([jnp.asarray(p, jnp.int32) for p in place])
    row_place = jnp.reshape(row, (1,)).astype(jnp.int32)

    matrices = [jnp.stack([moves.to_odd(coarse_inverse), coarse_inverse])]
    matrices.append(moves.pair(matrices[0]))
    matrices.append(moves.relay(matrices[1]))

    flux, packed, kernel, inverse = products(
        trace, double_layer[0, 0], single_inverse[0, 0], selector, load=True
    )
    rows = moves.exchange(packed, face)
    state, coarse, wide, wide_rows = trace, None, None, None
    for iteration in range(ITERS):
        last = iteration == ITERS - 1
        residual, state, u, rhs = update(
            place, rows, flux, load, state, selector_t, basis, tall, coarse, wide, wide_rows
        )
        pieces = moves.gather_rows(jnp.concatenate([moves.to_odd(rhs), rhs]))
        if not last:
            entering = jnp.concatenate([u, tall], axis=1) if iteration == 0 else u
            flux, packed = products(entering, kernel, inverse, selector)
            rows = moves.exchange(packed, face)
            if iteration == 0:
                wide, wide_rows = flux[:, width:], rows[:, :, width:]
                flux, rows = flux[:, :width], rows[:, :, :width]
        partial = coarse_product(row_place, pieces, matrices[:1] if last else matrices)
        coarse = moves.sum_chips(partial)
    own = lax.dynamic_slice_in_dim(coarse[0], col * MODES, MODES)
    trace = (state + dot(tall[:, :MODES], own)).astype(bf16)
    return trace[None, None], residual[None, None]


def solution(mesh):
    placed = (
        P("sub", "col", None, None),
        P("sub", "col", None, None),
        P("sub", "col", None, None),
        P("sub", "col", None, None),
        P("sub", "col", None, None),
        P("sub", "col", None),
        P("sub", "col", None),
        P("sub", "col"),
    )
    return jax.shard_map(
        local,
        mesh=mesh,
        in_specs=placed,
        out_specs=(P("sub", "col", None, None), P("sub", "col", None, None)),
        check_vma=False,
    )
```

```python
import functools

import jax
import jax.numpy as jnp
from jax import lax
from jax.experimental import pallas as pl
from jax.experimental.pallas import tpu as pltpu
from jax.sharding import PartitionSpec as P

MODES = 64
ITERS = 3
LANES = 128

bf16 = jnp.bfloat16
f32 = jnp.float32
DIRECTIONS = ((-1, -1), (-1, 0), (-1, 1), (0, -1), (0, 1), (1, -1), (1, 0), (1, 1))
PACKED = ((4, 1), (2, 0), (7, 0), (3, 1), (0, 0), (5, 0), (6, 1), (1, 1))

vmem = pl.BlockSpec(memory_space=pltpu.VMEM)
smem = pl.BlockSpec(memory_space=pltpu.SMEM)
hbm = pl.BlockSpec(memory_space=pl.ANY)
shape_of = jax.ShapeDtypeStruct
params = pltpu.CompilerParams(vmem_limit_bytes=24 * 1024 * 1024)
large = pltpu.CompilerParams(vmem_limit_bytes=50 * 1024 * 1024)


def dot(a, b):
    return jnp.dot(a, b, preferred_element_type=f32)


def pick(face, sel_ref, flux_ref, packed_ref):
    at = 0
    for d, whole in PACKED:
        size = face if whole else face // 8
        rows = dot(sel_ref[d, :size, :], flux_ref[d * face : (d + 1) * face, :])
        packed_ref[at : at + size, :] = rows.astype(bf16)
        at += size


def load_kernel(face, chunk, ahead, u_ref, k_hbm, s_hbm, sel_ref, flux_ref, packed_ref, k_ref, s_ref, mixed, sems):
    count = u_ref.shape[0] // chunk
    copies = []
    for which, (source, target) in enumerate(((k_hbm, k_ref), (s_hbm, s_ref))):
        for i in range(count):
            rows = pl.ds(i * chunk, chunk)
            copies.append(pltpu.make_async_copy(source.at[rows], target.at[rows], sems.at[which, i]))
    for copy in copies[:ahead]:
        copy.start()
    u = u_ref[...]
    for i in range(2 * count):
        copies[i].wait()
        if i + ahead < 2 * count:
            copies[i + ahead].start()
        rows = pl.ds(i % count * chunk, chunk)
        if i < count:
            mixed[rows, :] = (0.5 * u_ref[rows, :].astype(f32) + dot(k_ref[rows, :], u)).astype(bf16)
        else:
            flux_ref[rows, :] = dot(s_ref[rows, :], mixed[...]).astype(bf16)
    pick(face, sel_ref, flux_ref, packed_ref)


def products_kernel(face, chunk, u_ref, k_ref, s_ref, sel_ref, flux_ref, packed_ref, k_out, s_out, mixed):
    u = u_ref[...]
    for i in range(u_ref.shape[0] // chunk):
        rows = pl.ds(i * chunk, chunk)
        mixed[rows, :] = (0.5 * u_ref[rows, :].astype(f32) + dot(k_ref[rows, :], u)).astype(bf16)
    m = mixed[...]
    for i in range(u_ref.shape[0] // chunk):
        rows = pl.ds(i * chunk, chunk)
        flux_ref[rows, :] = dot(s_ref[rows, :], m).astype(bf16)
    pick(face, sel_ref, flux_ref, packed_ref)


def products(u, kernel, inverse, selector, load=False):
    nodes, width = u.shape
    face = selector.shape[1]
    chunk = 256 if nodes % 256 == 0 else nodes
    scratch = [pltpu.VMEM((nodes, width), bf16)]
    body = functools.partial(products_kernel, face, chunk)
    if load:
        scratch += [pltpu.SemaphoreType.DMA((2, nodes // chunk))]
        body = functools.partial(load_kernel, face, chunk, 3)
    return pl.pallas_call(
        body,
        out_shape=[
            shape_of((nodes, width), bf16),
            shape_of((4 * (face + face // 8), width), bf16),
            pltpu.VMEM((nodes, nodes), bf16),
            pltpu.VMEM((nodes, nodes), bf16),
        ],
        in_specs=[vmem] + [hbm if load else vmem] * 2 + [vmem],
        out_specs=[vmem] * 4,
        scratch_shapes=scratch,
        input_output_aliases={} if load else {1: 2, 2: 3},
        compiler_params=large if load else params,
        cost_estimate=pl.CostEstimate(
            flops=4 * nodes * nodes * 2 * LANES, bytes_accessed=4 * nodes * nodes, transcendentals=0
        ),
        name="load_products" if load else "products",
    )(u, kernel, inverse, selector)


def update_kernel(face, first, place, rows_ref, flux_ref, load_ref, state_ref, selt_ref, basis_ref, tall_ref, c_ref, w_ref, wrows_ref, res_ref, u_ref, rhs_ref):
    corner = face // 8
    modes = basis_ref.shape[0]
    found = {4: (0, 0), 3: (1, 0), 6: (2, 0), 1: (3, 0)}
    found |= {7: (2, face), 5: (2, face + corner), 2: (3, face), 0: (3, face + corner)}
    flux = flux_ref[...].astype(f32)
    state = state_ref[...].astype(f32)
    if not first:
        start = pl.multiple_of(place[1], modes)
        own = c_ref[place[0], pl.ds(start, modes), :]
        flux = (flux + dot(w_ref[:, :modes], own)).astype(bf16).astype(f32)
        state = state + dot(tall_ref[:, :modes], own)
    assembled = []
    for d in range(8):
        group, at = found[d]
        size = face if DIRECTIONS[d][0] * DIRECTIONS[d][1] == 0 else corner
        arrived = rows_ref[group, at : at + size, :]
        if not first:
            start = pl.multiple_of(place[2 * d + 3], modes)
            theirs = c_ref[place[2 * d + 2], pl.ds(start, modes), :]
            wide = wrows_ref[group, at : at + size, :modes]
            arrived = (arrived.astype(f32) + dot(wide, theirs)).astype(bf16)
        assembled.append(flux[d * face : (d + 1) * face] + dot(selt_ref[d, :, :size], arrived))
    assembled.append(flux[8 * face :])
    residual = (load_ref[...].astype(f32) - jnp.concatenate(assembled)).astype(bf16)
    res_ref[...] = residual
    following = state + 0.25 * residual.astype(f32)
    u_ref[...] = following.astype(bf16)
    rhs_ref[...] = dot(basis_ref[...], residual).astype(bf16)


def update(place, rows, flux, load, state, selector_t, basis, tall, coarse, wide, wide_rows):
    first = coarse is None
    nodes, width = load.shape
    modes = basis.shape[0]
    operands = [place, rows, flux, load, state, selector_t, basis, tall]
    body = functools.partial(update_kernel, selector_t.shape[1], first)
    if first:
        inner = body
        body = lambda *refs: inner(*refs[:8], None, None, None, *refs[8:])
    else:
        operands += [coarse, wide, wide_rows]
    return pl.pallas_call(
        body,
        out_shape=[
            shape_of((nodes, width), bf16),
            shape_of((nodes, width), bf16),
            shape_of((modes, width), bf16),
        ],
        in_specs=[smem] + [vmem] * (len(operands) - 1),
        out_specs=[vmem] * 3,
        compiler_params=params,
        cost_estimate=pl.CostEstimate(
            flops=8 * nodes * LANES * width, bytes_accessed=12 * nodes * width, transcendentals=0
        ),
        name="update",
    )(*operands)


def coarse_kernel(modes, place, pieces_ref, *refs):
    matrices, out_ref, full = refs[:-2], refs[-2], refs[-1]
    for m in range(pieces_ref.shape[0]):
        start = pl.multiple_of((place[0] ^ m) * modes, modes)
        full[pl.ds(start, modes), :] = pieces_ref[m]
    for i, matrix in enumerate(matrices):
        out_ref[i] = dot(matrix[...], full[...])


def coarse_product(place, pieces, matrices):
    count, modes, width = pieces.shape
    rows, depth = matrices[0].shape
    return pl.pallas_call(
        functools.partial(coarse_kernel, modes),
        out_shape=shape_of((len(matrices), rows, width), f32),
        in_specs=[smem] + [vmem] * (1 + len(matrices)),
        out_specs=vmem,
        scratch_shapes=[pltpu.VMEM((depth, width), bf16)],
        compiler_params=params,
        cost_estimate=pl.CostEstimate(
            flops=2 * len(matrices) * rows * depth * width,
            bytes_accessed=2 * len(matrices) * rows * depth,
            transcendentals=0,
        ),
        name="coarse_product",
    )(place, pieces, *matrices)


def swap(value, axis, bit):
    return lax.ppermute(value, axis, [(i, i ^ bit) for i in range(lax.axis_size(axis))])


def cross(value, axis):
    n = lax.axis_size(axis)
    return lax.ppermute(value, axis, [(i, (i + 1 if i % 2 else i - 1) % n) for i in range(n)])


def trade(forward, backward, axis):
    even = lax.axis_index(axis) % 2 == 0
    near = swap(jnp.where(even, forward, backward), axis, 1)
    far = cross(jnp.where(even, backward, forward), axis)
    return jnp.where(even, near, far), jnp.where(even, far, near)


def exchange(packed, face):
    corner = face // 8
    group = face + 2 * corner
    right, left = trade(packed[:group], packed[group : 2 * group], "col")
    six, one = packed[2 * group : 2 * group + face], packed[2 * group + face :]
    up = jnp.concatenate([six, right[face + corner :], left[face + corner :]])
    down = jnp.concatenate([one, right[face : face + corner], left[face : face + corner]])
    above, below = trade(up, down, "sub")
    return jnp.stack([right, left, above, below])


def sum_over_columns(value):
    bit = lax.axis_size("col") // 2
    while bit:
        value = value + swap(value.astype(bf16), "col", bit).astype(f32)
        bit //= 2
    return value.astype(bf16)


def share_of_sum(value):
    bit = lax.axis_size("col") // 2
    while bit:
        half = value.shape[0] // 2
        upper = (lax.axis_index("col") // bit) % 2 == 1
        low, high = value[:half], value[half:]
        got = swap(jnp.where(upper, low, high).astype(bf16), "col", bit)
        value = jnp.where(upper, high, low) + got.astype(f32)
        bit //= 2
    return value.astype(bf16)


def local(
    trace_start,
    neumann_load,
    double_layer,
    single_inverse,
    interface_nodes,
    node_mode,
    mode_weight,
    coarse_inverse,
):
    subs, cols = lax.axis_size("sub"), lax.axis_size("col")
    row, col = lax.axis_index("sub"), lax.axis_index("col")
    even_sub = row % 2 == 0
    trace = trace_start[0, 0]
    load = neumann_load[0, 0]
    width = trace.shape[1]
    interface = interface_nodes[0, 0]
    face = interface.shape[1]
    position = interface - (jnp.arange(8, dtype=jnp.int32) * face)[:, None]
    slots = jnp.arange(face, dtype=jnp.int32)
    selector = (position[:, :, None] == slots[None, None, :]).astype(bf16)
    selector_t = (position[:, None, :] == slots[None, :, None]).astype(bf16)
    nothing = jnp.zeros((), bf16)
    mode, weight = node_mode[0, 0], mode_weight[0, 0]
    modes = jnp.arange(MODES, dtype=jnp.int32)
    lanes = jnp.arange(LANES, dtype=jnp.int32)
    basis = jnp.where(mode[None, :] == modes[:, None], weight[None, :], nothing)
    tall = jnp.where(mode[:, None] == lanes[None, :], weight[:, None], nothing)

    place = [jnp.zeros((), jnp.int32), col * MODES]
    for row_step, col_step in DIRECTIONS:
        source = {0: 0, 1: jnp.where(even_sub, 1, 2), -1: jnp.where(even_sub, 2, 1)}
        place += [source[row_step], jnp.clip(col + col_step, 0, cols - 1) * MODES]
    place = jnp.stack([jnp.asarray(p, jnp.int32) for p in place])
    row_place = jnp.reshape(row, (1,)).astype(jnp.int32)

    matrices = [coarse_inverse, swap(coarse_inverse, "sub", 1), cross(coarse_inverse, "sub")]

    flux, packed, kernel, inverse = products(
        trace, double_layer[0, 0], single_inverse[0, 0], selector, load=True
    )
    rows = exchange(packed, face)
    u, coarse, wide, wide_rows = trace, None, None, None
    for iteration in range(ITERS):
        last = iteration == ITERS - 1
        residual, u, rhs = update(
            place, rows, flux, load, u, selector_t, basis, tall, coarse, wide, wide_rows
        )
        got = swap(rhs, "sub", 1)
        pieces = jnp.stack([rhs, got])
        if not last:
            entering, pieces = lax.optimization_barrier((u, pieces))
            if iteration == 0:
                entering = jnp.concatenate([entering, tall], axis=1)
            flux, packed, kernel, inverse = products(entering, kernel, inverse, selector)
            rows = exchange(packed, face)
            if iteration == 0:
                wide, wide_rows = flux[:, width:], rows[:, :, width:]
                flux, rows = flux[:, :width], rows[:, :, :width]
        while pieces.shape[0] < subs:
            got = swap(pieces, "sub", pieces.shape[0])
            pieces = jnp.concatenate([pieces, got])
        if last:
            own = share_of_sum(coarse_product(row_place, pieces, matrices[:1])[0])
        else:
            coarse = sum_over_columns(coarse_product(row_place, pieces, matrices))
    trace = (u.astype(f32) + dot(tall[:, :MODES], own)).astype(bf16)
    return trace[None, None], residual[None, None]


def solution(mesh):
    placed = (
        P("sub", "col", None, None),
        P("sub", "col", None, None),
        P("sub", "col", None, None),
        P("sub", "col", None, None),
        P("sub", "col", None, None),
        P("sub", "col", None),
        P("sub", "col", None),
        P("sub", "col"),
    )
    return jax.shard_map(
        local,
        mesh=mesh,
        in_specs=placed,
        out_specs=(P("sub", "col", None, None), P("sub", "col", None, None)),
        check_vma=False,
    )
```

```python
import functools

import jax
import jax.numpy as jnp
from jax import lax
from jax.experimental import pallas as pl
from jax.experimental.pallas import tpu as pltpu
from jax.sharding import PartitionSpec as P

MODES = 64
ITERS = 3
LANES = 128

bf16 = jnp.bfloat16
f32 = jnp.float32
DIRECTIONS = ((-1, -1), (-1, 0), (-1, 1), (0, -1), (0, 1), (1, -1), (1, 0), (1, 1))
PACKED = ((4, 1), (2, 0), (7, 0), (3, 1), (0, 0), (5, 0), (6, 1), (1, 1))

vmem = pl.BlockSpec(memory_space=pltpu.VMEM)
smem = pl.BlockSpec(memory_space=pltpu.SMEM)
hbm = pl.BlockSpec(memory_space=pl.ANY)
shape_of = jax.ShapeDtypeStruct
params = pltpu.CompilerParams(vmem_limit_bytes=16 * 1024 * 1024)
large = pltpu.CompilerParams(vmem_limit_bytes=50 * 1024 * 1024)


def dot(a, b):
    return jnp.dot(a, b, preferred_element_type=f32)


def pick(face, sel_ref, flux_ref, packed_ref):
    at = 0
    for d, whole in PACKED:
        size = face if whole else face // 8
        rows = dot(sel_ref[d, :size, :], flux_ref[d * face : (d + 1) * face, :])
        packed_ref[at : at + size, :] = rows.astype(bf16)
        at += size


def load_kernel(face, chunk, ahead, u_ref, k_hbm, s_hbm, sel_ref, flux_ref, packed_ref, mixed, k_ref, s_ref, sems):
    count = u_ref.shape[0] // chunk
    copies = []
    for which, (source, target) in enumerate(((k_hbm, k_ref), (s_hbm, s_ref))):
        for i in range(count):
            rows = pl.ds(i * chunk, chunk)
            copies.append(pltpu.make_async_copy(source.at[rows], target.at[rows], sems.at[which, i]))
    for copy in copies[:ahead]:
        copy.start()
    u = u_ref[...]
    for i in range(2 * count):
        copies[i].wait()
        if i + ahead < 2 * count:
            copies[i + ahead].start()
        rows = pl.ds(i % count * chunk, chunk)
        if i < count:
            mixed[rows, :] = (0.5 * u_ref[rows, :].astype(f32) + dot(k_ref[rows, :], u)).astype(bf16)
        else:
            flux_ref[rows, :] = dot(s_ref[rows, :], mixed[...]).astype(bf16)
    pick(face, sel_ref, flux_ref, packed_ref)


def products_kernel(face, chunk, u_ref, k_ref, s_ref, sel_ref, flux_ref, packed_ref, mixed):
    u = u_ref[...]
    for i in range(u_ref.shape[0] // chunk):
        rows = pl.ds(i * chunk, chunk)
        mixed[rows, :] = (0.5 * u_ref[rows, :].astype(f32) + dot(k_ref[rows, :], u)).astype(bf16)
    m = mixed[...]
    for i in range(u_ref.shape[0] // chunk):
        rows = pl.ds(i * chunk, chunk)
        flux_ref[rows, :] = dot(s_ref[rows, :], m).astype(bf16)
    pick(face, sel_ref, flux_ref, packed_ref)


def products(u, kernel, inverse, selector, load=False):
    nodes, width = u.shape
    face = selector.shape[1]
    chunk = 256 if nodes % 256 == 0 else nodes
    scratch = [pltpu.VMEM((nodes, width), bf16)]
    body = functools.partial(products_kernel, face, chunk)
    if load:
        scratch += [pltpu.VMEM((nodes, nodes), bf16)] * 2
        scratch += [pltpu.SemaphoreType.DMA((2, nodes // chunk))]
        body = functools.partial(load_kernel, face, chunk, 3)
    return pl.pallas_call(
        body,
        out_shape=[
            shape_of((nodes, width), bf16),
            shape_of((4 * (face + face // 8), width), bf16),
        ],
        in_specs=[vmem] + [hbm if load else vmem] * 2 + [vmem],
        out_specs=[vmem] * 2,
        scratch_shapes=scratch,
        compiler_params=large if load else params,
        cost_estimate=pl.CostEstimate(
            flops=4 * nodes * nodes * 2 * LANES, bytes_accessed=4 * nodes * nodes, transcendentals=0
        ),
        name="load_products" if load else "products",
    )(u, kernel, inverse, selector)


def update_kernel(face, first, place, rows_ref, flux_ref, load_ref, state_ref, selt_ref, basis_ref, tall_ref, c_ref, w_ref, wrows_ref, res_ref, u_ref, rhs_ref):
    corner = face // 8
    modes = basis_ref.shape[0]
    found = {4: (0, 0), 3: (1, 0), 6: (2, 0), 1: (3, 0)}
    found |= {7: (2, face), 5: (2, face + corner), 2: (3, face), 0: (3, face + corner)}
    flux = flux_ref[...].astype(f32)
    state = state_ref[...].astype(f32)
    if not first:
        start = pl.multiple_of(place[1], modes)
        own = c_ref[place[0], pl.ds(start, modes), :]
        flux = (flux + dot(w_ref[:, :modes], own)).astype(bf16).astype(f32)
        state = state + dot(tall_ref[:, :modes], own)
    assembled = []
    for d in range(8):
        group, at = found[d]
        size = face if DIRECTIONS[d][0] * DIRECTIONS[d][1] == 0 else corner
        arrived = rows_ref[group, at : at + size, :]
        if not first:
            start = pl.multiple_of(place[2 * d + 3], modes)
            theirs = c_ref[place[2 * d + 2], pl.ds(start, modes), :]
            wide = wrows_ref[group, at : at + size, :modes]
            arrived = (arrived.astype(f32) + dot(wide, theirs)).astype(bf16)
        assembled.append(flux[d * face : (d + 1) * face] + dot(selt_ref[d, :, :size], arrived))
    assembled.append(flux[8 * face :])
    residual = (load_ref[...].astype(f32) - jnp.concatenate(assembled)).astype(bf16)
    res_ref[...] = residual
    following = state + 0.25 * residual.astype(f32)
    u_ref[...] = following.astype(bf16)
    rhs_ref[...] = dot(basis_ref[...], residual).astype(bf16)


def update(place, rows, flux, load, state, selector_t, basis, tall, coarse, wide, wide_rows):
    first = coarse is None
    nodes, width = load.shape
    modes = basis.shape[0]
    operands = [place, rows, flux, load, state, selector_t, basis, tall]
    body = functools.partial(update_kernel, selector_t.shape[1], first)
    if first:
        inner = body
        body = lambda *refs: inner(*refs[:8], None, None, None, *refs[8:])
    else:
        operands += [coarse, wide, wide_rows]
    return pl.pallas_call(
        body,
        out_shape=[
            shape_of((nodes, width), bf16),
            shape_of((nodes, width), bf16),
            shape_of((modes, width), bf16),
        ],
        in_specs=[smem] + [vmem] * (len(operands) - 1),
        out_specs=[vmem] * 3,
        compiler_params=params,
        cost_estimate=pl.CostEstimate(
            flops=8 * nodes * LANES * width, bytes_accessed=12 * nodes * width, transcendentals=0
        ),
        name="update",
    )(*operands)


def coarse_kernel(modes, place, pieces_ref, *refs):
    matrices, out_ref, full = refs[:-2], refs[-2], refs[-1]
    for m in range(pieces_ref.shape[0]):
        start = pl.multiple_of((place[0] ^ m) * modes, modes)
        full[pl.ds(start, modes), :] = pieces_ref[m]
    for i, matrix in enumerate(matrices):
        out_ref[i] = dot(matrix[...], full[...])


def coarse_product(place, pieces, matrices):
    count, modes, width = pieces.shape
    rows, depth = matrices[0].shape
    return pl.pallas_call(
        functools.partial(coarse_kernel, modes),
        out_shape=shape_of((len(matrices), rows, width), f32),
        in_specs=[smem] + [vmem] * (1 + len(matrices)),
        out_specs=vmem,
        scratch_shapes=[pltpu.VMEM((depth, width), bf16)],
        compiler_params=params,
        cost_estimate=pl.CostEstimate(
            flops=2 * len(matrices) * rows * depth * width,
            bytes_accessed=2 * len(matrices) * rows * depth,
            transcendentals=0,
        ),
        name="coarse_product",
    )(place, pieces, *matrices)


def swap(value, axis, bit):
    return lax.ppermute(value, axis, [(i, i ^ bit) for i in range(lax.axis_size(axis))])


def cross(value, axis):
    n = lax.axis_size(axis)
    return lax.ppermute(value, axis, [(i, (i + 1 if i % 2 else i - 1) % n) for i in range(n)])


def trade(forward, backward, axis):
    even = lax.axis_index(axis) % 2 == 0
    near = swap(jnp.where(even, forward, backward), axis, 1)
    far = cross(jnp.where(even, backward, forward), axis)
    return jnp.where(even, near, far), jnp.where(even, far, near)


def exchange(packed, face):
    corner = face // 8
    group = face + 2 * corner
    right, left = trade(packed[:group], packed[group : 2 * group], "col")
    six, one = packed[2 * group : 2 * group + face], packed[2 * group + face :]
    up = jnp.concatenate([six, right[face + corner :], left[face + corner :]])
    down = jnp.concatenate([one, right[face : face + corner], left[face : face + corner]])
    above, below = trade(up, down, "sub")
    return jnp.stack([right, left, above, below])


def sum_over_columns(value):
    bit = lax.axis_size("col") // 2
    while bit:
        value = value + swap(value.astype(bf16), "col", bit).astype(f32)
        bit //= 2
    return value.astype(bf16)


def share_of_sum(value):
    bit = lax.axis_size("col") // 2
    while bit:
        half = value.shape[0] // 2
        upper = (lax.axis_index("col") // bit) % 2 == 1
        low, high = value[:half], value[half:]
        got = swap(jnp.where(upper, low, high).astype(bf16), "col", bit)
        value = jnp.where(upper, high, low) + got.astype(f32)
        bit //= 2
    return value.astype(bf16)


def local(
    trace_start,
    neumann_load,
    double_layer,
    single_inverse,
    interface_nodes,
    node_mode,
    mode_weight,
    coarse_inverse,
):
    subs, cols = lax.axis_size("sub"), lax.axis_size("col")
    row, col = lax.axis_index("sub"), lax.axis_index("col")
    even_sub = row % 2 == 0
    trace = trace_start[0, 0]
    load = neumann_load[0, 0]
    width = trace.shape[1]
    interface = interface_nodes[0, 0]
    face = interface.shape[1]
    position = interface - (jnp.arange(8, dtype=jnp.int32) * face)[:, None]
    slots = jnp.arange(face, dtype=jnp.int32)
    selector = (position[:, :, None] == slots[None, None, :]).astype(bf16)
    selector_t = (position[:, None, :] == slots[None, :, None]).astype(bf16)
    nothing = jnp.zeros((), bf16)
    mode, weight = node_mode[0, 0], mode_weight[0, 0]
    modes = jnp.arange(MODES, dtype=jnp.int32)
    lanes = jnp.arange(LANES, dtype=jnp.int32)
    basis = jnp.where(mode[None, :] == modes[:, None], weight[None, :], nothing)
    tall = jnp.where(mode[:, None] == lanes[None, :], weight[:, None], nothing)

    place = [jnp.zeros((), jnp.int32), col * MODES]
    for row_step, col_step in DIRECTIONS:
        source = {0: 0, 1: jnp.where(even_sub, 1, 2), -1: jnp.where(even_sub, 2, 1)}
        place += [source[row_step], jnp.clip(col + col_step, 0, cols - 1) * MODES]
    place = jnp.stack([jnp.asarray(p, jnp.int32) for p in place])
    row_place = jnp.reshape(row, (1,)).astype(jnp.int32)

    matrices = [coarse_inverse, swap(coarse_inverse, "sub", 1), cross(coarse_inverse, "sub")]

    kernel, inverse = double_layer[0, 0], single_inverse[0, 0]
    flux, packed = products(trace, kernel, inverse, selector, load=True)
    rows = exchange(packed, face)
    u, coarse, wide, wide_rows = trace, None, None, None
    for iteration in range(ITERS):
        last = iteration == ITERS - 1
        residual, u, rhs = update(
            place, rows, flux, load, u, selector_t, basis, tall, coarse, wide, wide_rows
        )
        got = swap(rhs, "sub", 1)
        pieces = jnp.stack([rhs, got])
        if not last:
            entering, pieces = lax.optimization_barrier((u, pieces))
            if iteration == 0:
                entering = jnp.concatenate([entering, tall], axis=1)
            flux, packed = products(entering, kernel, inverse, selector)
            rows = exchange(packed, face)
            if iteration == 0:
                wide, wide_rows = flux[:, width:], rows[:, :, width:]
                flux, rows = flux[:, :width], rows[:, :, :width]
        while pieces.shape[0] < subs:
            got = swap(pieces, "sub", pieces.shape[0])
            pieces = jnp.concatenate([pieces, got])
        if last:
            own = share_of_sum(coarse_product(row_place, pieces, matrices[:1])[0])
        else:
            coarse = sum_over_columns(coarse_product(row_place, pieces, matrices))
    trace = (u.astype(f32) + dot(tall[:, :MODES], own)).astype(bf16)
    return trace[None, None], residual[None, None]


def solution(mesh):
    placed = (
        P("sub", "col", None, None),
        P("sub", "col", None, None),
        P("sub", "col", None, None),
        P("sub", "col", None, None),
        P("sub", "col", None, None),
        P("sub", "col", None),
        P("sub", "col", None),
        P("sub", "col"),
    )
    return jax.shard_map(
        local,
        mesh=mesh,
        in_specs=placed,
        out_specs=(P("sub", "col", None, None), P("sub", "col", None, None)),
        check_vma=False,
    )
```

```python
import functools

import jax
import jax.numpy as jnp
from jax import lax
from jax.experimental import pallas as pl
from jax.experimental.pallas import tpu as pltpu
from jax.sharding import PartitionSpec as P

MODES = 64
ITERS = 3
LANES = 128

bf16 = jnp.bfloat16
f32 = jnp.float32
DIRECTIONS = ((-1, -1), (-1, 0), (-1, 1), (0, -1), (0, 1), (1, -1), (1, 0), (1, 1))
PACKED = ((4, 1), (2, 0), (7, 0), (3, 1), (0, 0), (5, 0), (6, 1), (1, 1))

vmem = pl.BlockSpec(memory_space=pltpu.VMEM)
smem = pl.BlockSpec(memory_space=pltpu.SMEM)
hbm = pl.BlockSpec(memory_space=pl.ANY)
shape_of = jax.ShapeDtypeStruct
params = pltpu.CompilerParams(vmem_limit_bytes=16 * 1024 * 1024)
large = pltpu.CompilerParams(vmem_limit_bytes=16 * 1024 * 1024)


def dot(a, b):
    return jnp.dot(a, b, preferred_element_type=f32)


def pick(face, sel_ref, flux_ref, packed_ref):
    at = 0
    for d, whole in PACKED:
        size = face if whole else face // 8
        rows = dot(sel_ref[d, :size, :], flux_ref[d * face : (d + 1) * face, :])
        packed_ref[at : at + size, :] = rows.astype(bf16)
        at += size


def load_kernel(face, chunk, ahead, u_hbm, k_hbm, s_hbm, nodes_hbm, mode_hbm, weight_ref, flux_ref, packed_ref, sel_ref, selt_ref, basis_ref, tall_ref, k_ref, s_ref, mixed, u_ref, nodes_ref, mode_ref, sems, small_sems):
    count = u_ref.shape[0] // chunk
    small = ((u_hbm, u_ref), (nodes_hbm, nodes_ref), (mode_hbm, mode_ref))
    small = [pltpu.make_async_copy(*pair, small_sems.at[i]) for i, pair in enumerate(small)]
    for copy in small:
        copy.start()
    copies = []
    for which, (source, target) in enumerate(((k_hbm, k_ref), (s_hbm, s_ref))):
        for i in range(count):
            rows = pl.ds(i * chunk, chunk)
            copies.append(pltpu.make_async_copy(source.at[rows], target.at[rows], sems.at[which, i]))
    for copy in copies[:ahead]:
        copy.start()
    modes = basis_ref.shape[0]
    slot = lax.broadcasted_iota(jnp.int32, (face, face), 0)
    mode = lax.broadcasted_iota(jnp.int32, (modes, LANES), 0)
    blocks = u_ref.shape[0] // LANES

    def prepare(step, steps):
        for d in range(8 * step // steps, 8 * (step + 1) // steps):
            chosen = (slot == nodes_ref[d : d + 1, :] - d * face).astype(f32)
            selt_ref[d] = chosen.astype(bf16)
            sel_ref[d] = chosen.T.astype(bf16)
        for i in range(blocks * step // steps, blocks * (step + 1) // steps):
            rows = pl.ds(i * LANES, LANES)
            part = jnp.where(mode == mode_ref[:, rows], weight_ref[:, rows].astype(f32), 0.0)
            basis_ref[:, rows] = part.astype(bf16)
            tall_ref[rows, :] = jnp.concatenate([part] * (LANES // modes)).T.astype(bf16)

    for copy in small:
        copy.wait()
    u = u_ref[...]
    for i in range(2 * count):
        prepare(i, 2 * count)
        copies[i].wait()
        if i + ahead < 2 * count:
            copies[i + ahead].start()
        rows = pl.ds(i % count * chunk, chunk)
        if i < count:
            mixed[rows, :] = (0.5 * u_ref[rows, :].astype(f32) + dot(k_ref[rows, :], u)).astype(bf16)
        else:
            flux_ref[rows, :] = dot(s_ref[rows, :], mixed[...]).astype(bf16)
    pick(face, sel_ref, flux_ref, packed_ref)


def load_products(trace, kernel, inverse, nodes, mode, weight):
    count, width = trace.shape
    face = nodes.shape[1]
    chunk = 256 if count % 256 == 0 else count
    return pl.pallas_call(
        functools.partial(load_kernel, face, chunk, 3),
        out_shape=[
            shape_of((count, width), bf16),
            shape_of((4 * (face + face // 8), width), bf16),
            shape_of((8, face, face), bf16),
            shape_of((8, face, face), bf16),
            shape_of((MODES, count), bf16),
            shape_of((count, LANES), bf16),
            pltpu.VMEM((count, count), bf16),
            pltpu.VMEM((count, count), bf16),
        ],
        in_specs=[hbm] * 5 + [vmem],
        out_specs=[vmem] * 8,
        scratch_shapes=[
            pltpu.VMEM((count, width), bf16),
            pltpu.VMEM((count, width), bf16),
            pltpu.VMEM(nodes.shape, jnp.int32),
            pltpu.VMEM(mode.shape, jnp.int32),
            pltpu.SemaphoreType.DMA((2, count // chunk)),
            pltpu.SemaphoreType.DMA((3,)),
        ],
        compiler_params=large,
        cost_estimate=pl.CostEstimate(
            flops=4 * count * count * 2 * LANES, bytes_accessed=4 * count * count, transcendentals=0
        ),
        name="load_products",
    )(trace, kernel, inverse, nodes, mode, weight)


def products_kernel(face, chunk, state_ref, res_ref, k_ref, s_ref, sel_ref, tall_ref, c_ref, u_ref, flux_ref, packed_ref, entering, mixed):
    count, width = u_ref.shape
    for i in range(count // chunk):
        rows = pl.ds(i * chunk, chunk)
        following = state_ref[rows, :].astype(f32) + 0.25 * res_ref[rows, :].astype(f32)
        if c_ref is not None:
            following += dot(tall_ref[rows, : c_ref.shape[0]], c_ref[...])
        u_ref[rows, :] = following.astype(bf16)
        entering[rows, :width] = following.astype(bf16)
        if c_ref is None:
            entering[rows, width:] = tall_ref[rows, :]
    u = entering[...]
    for i in range(count // chunk):
        rows = pl.ds(i * chunk, chunk)
        mixed[rows, :] = (0.5 * entering[rows, :].astype(f32) + dot(k_ref[rows, :], u)).astype(bf16)
    m = mixed[...]
    for i in range(count // chunk):
        rows = pl.ds(i * chunk, chunk)
        flux_ref[rows, :] = dot(s_ref[rows, :], m).astype(bf16)
    pick(face, sel_ref, flux_ref, packed_ref)


def products(state, residual, kernel, inverse, selector, tall, own):
    count, width = state.shape
    face = selector.shape[1]
    chunk = 256 if count % 256 == 0 else count
    wide = width + LANES if own is None else width
    operands = [state, residual, kernel, inverse, selector, tall]
    body = functools.partial(products_kernel, face, chunk)
    if own is None:
        inner = body
        body = lambda *refs: inner(*refs[:6], None, *refs[6:])
    else:
        operands.append(own)
    return pl.pallas_call(
        body,
        out_shape=[
            shape_of((count, width), bf16),
            shape_of((count, wide), bf16),
            shape_of((4 * (face + face // 8), wide), bf16),
        ],
        in_specs=[vmem] * len(operands),
        out_specs=[vmem] * 3,
        scratch_shapes=[pltpu.VMEM((count, wide), bf16), pltpu.VMEM((count, wide), bf16)],
        compiler_params=params,
        cost_estimate=pl.CostEstimate(
            flops=4 * count * count * 2 * LANES, bytes_accessed=4 * count * count, transcendentals=0
        ),
        name="products",
    )(*operands)


def arrivals(face):
    corner = face // 8
    found = {4: (0, 0), 3: (1, 0), 6: (2, 0), 1: (3, 0)}
    found |= {7: (2, face), 5: (2, face + corner), 2: (3, face), 0: (3, face + corner)}
    return [found[d] + (face if d in (1, 3, 4, 6) else corner,) for d in range(8)]


def couple_kernel(modes, selt_ref, w_ref, wrows_ref, out_ref):
    face = selt_ref.shape[1]
    lane = lax.broadcasted_iota(jnp.int32, (face, LANES), 1)
    for d, (group, at, size) in enumerate(arrivals(face)):
        theirs = dot(selt_ref[d, :, :size], wrows_ref[group, at : at + size, :])
        mine = w_ref[d * face : (d + 1) * face, :].astype(f32)
        out_ref[d, :, :face] = selt_ref[d]
        out_ref[d, :, face:] = jnp.where(lane < modes, theirs, mine).astype(bf16)


def couple(selector_t, wide, wide_rows):
    face = selector_t.shape[1]
    return pl.pallas_call(
        functools.partial(couple_kernel, MODES),
        out_shape=shape_of((8, face, face + LANES), bf16),
        in_specs=[vmem] * 3,
        out_specs=vmem,
        compiler_params=params,
        name="couple",
    )(selector_t, wide, wide_rows)


def first_update_kernel(rows_ref, flux_ref, load_ref, selt_ref, basis_ref, res_ref, rhs_ref):
    face = selt_ref.shape[1]
    for d, (group, at, size) in enumerate(arrivals(face)):
        band = slice(d * face, (d + 1) * face)
        placed = dot(selt_ref[d, :, :size], rows_ref[group, at : at + size, :])
        assembled = flux_ref[band, :].astype(f32) + placed
        res_ref[band, :] = (load_ref[band, :].astype(f32) - assembled).astype(bf16)
    rest = slice(8 * face, None)
    res_ref[rest, :] = (load_ref[rest, :].astype(f32) - flux_ref[rest, :].astype(f32)).astype(bf16)
    rhs_ref[...] = dot(basis_ref[...], res_ref[...]).astype(bf16)


def update_kernel(place, rows_ref, flux_ref, load_ref, couple_ref, basis_ref, c_ref, w_ref, res_ref, rhs_ref, own_ref, right):
    face = couple_ref.shape[1]
    modes = basis_ref.shape[0]
    own = c_ref[place[0], pl.ds(pl.multiple_of(place[1], modes), modes), :]
    own_ref[...] = own
    for d, (group, at, size) in enumerate(arrivals(face)):
        band = slice(d * face, (d + 1) * face)
        start = pl.multiple_of(place[2 * d + 3], modes)
        right[d, :size, :] = rows_ref[group, at : at + size, :]
        if size < face:
            right[d, size:face, :] = jnp.zeros((face - size, right.shape[2]), bf16)
        right[d, face : face + modes, :] = c_ref[place[2 * d + 2], pl.ds(start, modes), :]
        right[d, face + modes :, :] = own
        assembled = flux_ref[band, :].astype(f32) + dot(couple_ref[d], right[d])
        res_ref[band, :] = (load_ref[band, :].astype(f32) - assembled).astype(bf16)
    rest = slice(8 * face, None)
    assembled = flux_ref[rest, :].astype(f32) + dot(w_ref[rest, :modes], own)
    res_ref[rest, :] = (load_ref[rest, :].astype(f32) - assembled).astype(bf16)
    rhs = dot(basis_ref[...], res_ref[...]).astype(bf16)
    for i in range(rhs_ref.shape[0] // modes):
        rhs_ref[i * modes : (i + 1) * modes, :] = rhs


def settle_kernel(state_ref, res_ref, tall_ref, own_ref, out_ref, before_ref):
    res = res_ref[...]
    out_ref[...] = res
    product = dot(tall_ref[:, : own_ref.shape[0]], own_ref[...])
    before_ref[...] = state_ref[...].astype(f32) + 0.25 * res.astype(f32) + product


def settle(state, residual, tall, own):
    return pl.pallas_call(
        settle_kernel,
        out_shape=[shape_of(state.shape, bf16), shape_of(state.shape, f32)],
        in_specs=[vmem] * 4,
        out_specs=[vmem] * 2,
        compiler_params=params,
        name="settle",
    )(state, residual, tall, own)


def finish_kernel(before_ref, tall_ref, own_ref, trace_ref):
    trace_ref[...] = (before_ref[...] + dot(tall_ref[:, : own_ref.shape[0]], own_ref[...])).astype(bf16)


def finish(before, tall, own):
    return pl.pallas_call(
        finish_kernel,
        out_shape=shape_of(before.shape, bf16),
        in_specs=[vmem] * 3,
        out_specs=vmem,
        compiler_params=params,
        name="finish",
    )(before, tall, own)


def update(place, rows, flux, load, selector_t, basis, coarse, wide, coupling, copies=1):
    count, width = load.shape
    modes = basis.shape[0]
    face = selector_t.shape[1]
    outs = [shape_of((count, width), bf16), shape_of((copies * modes, width), bf16)]
    if coarse is None:
        operands = [rows, flux, load, selector_t, basis]
        return pl.pallas_call(
            first_update_kernel,
            out_shape=outs,
            in_specs=[vmem] * 5,
            out_specs=[vmem] * 2,
            compiler_params=params,
            name="first_update",
        )(*operands)
    operands = [place, rows, flux, load, coupling, basis, coarse, wide]
    return pl.pallas_call(
        update_kernel,
        out_shape=outs + [shape_of((modes, width), bf16)],
        in_specs=[smem] + [vmem] * 7,
        out_specs=[vmem] * 3,
        scratch_shapes=[pltpu.VMEM((8, face + LANES, width), bf16)],
        compiler_params=params,
        name="update",
    )(*operands)


def coarse_kernel(modes, place, pieces_ref, *refs):
    matrices, out_ref, full = refs[:-2], refs[-2], refs[-1]
    for m in range(pieces_ref.shape[0]):
        start = pl.multiple_of((place[0] ^ m) * modes, modes)
        full[pl.ds(start, modes), :] = pieces_ref[m]
    for i, matrix in enumerate(matrices):
        out_ref[i] = dot(matrix[...], full[...])


def coarse_product(place, pieces, matrices):
    count, modes, width = pieces.shape
    rows, depth = matrices[0].shape
    return pl.pallas_call(
        functools.partial(coarse_kernel, modes),
        out_shape=shape_of((len(matrices), rows, width), f32),
        in_specs=[smem] + [vmem] * (1 + len(matrices)),
        out_specs=vmem,
        scratch_shapes=[pltpu.VMEM((depth, width), bf16)],
        compiler_params=params,
        cost_estimate=pl.CostEstimate(
            flops=2 * len(matrices) * rows * depth * width,
            bytes_accessed=2 * len(matrices) * rows * depth,
            transcendentals=0,
        ),
        name="coarse_product",
    )(place, pieces, *matrices)


def swap(value, axis, bit):
    return lax.ppermute(value, axis, [(i, i ^ bit) for i in range(lax.axis_size(axis))])


def cross(value, axis):
    n = lax.axis_size(axis)
    return lax.ppermute(value, axis, [(i, (i + 1 if i % 2 else i - 1) % n) for i in range(n)])


def onward(value, axis):
    n = lax.axis_size(axis)
    ring = list(range(0, n, 2)) + list(range(n - 1, 0, -2))
    return lax.ppermute(value, axis, [(ring[i - 1], ring[i]) for i in range(n)])


def trade(forward, backward, axis):
    even = lax.axis_index(axis) % 2 == 0
    near = swap(jnp.where(even, forward, backward), axis, 1)
    far = cross(jnp.where(even, backward, forward), axis)
    return jnp.where(even, near, far), jnp.where(even, far, near)


def exchange(packed, face):
    corner = face // 8
    group = face + 2 * corner
    right, left = trade(packed[:group], packed[group : 2 * group], "col")
    six, one = packed[2 * group : 2 * group + face], packed[2 * group + face :]
    up = jnp.concatenate([six, right[face + corner :], left[face + corner :]])
    down = jnp.concatenate([one, right[face : face + corner], left[face : face + corner]])
    above, below = trade(up, down, "sub")
    return jnp.stack([right, left, above, below])


def sum_over_columns(value):
    bit = lax.axis_size("col") // 2
    while bit:
        value = value + swap(value.astype(bf16), "col", bit).astype(f32)
        bit //= 2
    return value.astype(bf16)


def share_of_sum(value):
    bit = lax.axis_size("col") // 2
    while bit:
        half = value.shape[0] // 2
        upper = (lax.axis_index("col") // bit) % 2 == 1
        low, high = value[:half], value[half:]
        got = swap(jnp.where(upper, low, high).astype(bf16), "col", bit)
        value = jnp.where(upper, high, low) + got.astype(f32)
        bit //= 2
    return value.astype(bf16)


def local(
    trace_start,
    neumann_load,
    double_layer,
    single_inverse,
    interface_nodes,
    node_mode,
    mode_weight,
    coarse_inverse,
):
    subs, cols = lax.axis_size("sub"), lax.axis_size("col")
    row, col = lax.axis_index("sub"), lax.axis_index("col")
    even_sub = row % 2 == 0
    trace = trace_start[0, 0]
    load = neumann_load[0, 0]
    width = trace.shape[1]
    interface = interface_nodes[0, 0]
    face = interface.shape[1]

    place = [jnp.zeros((), jnp.int32), col * MODES]
    for row_step, col_step in DIRECTIONS:
        source = {0: 0, 1: jnp.where(even_sub, 1, 2), -1: jnp.where(even_sub, 2, 1)}
        place += [source[row_step], jnp.clip(col + col_step, 0, cols - 1) * MODES]
    place = jnp.stack([jnp.asarray(p, jnp.int32) for p in place])
    row_place = jnp.reshape(row, (1,)).astype(jnp.int32)
    trace, place, row_place = lax.optimization_barrier((trace, place, row_place))

    flux, packed, selector, selector_t, basis, tall, kernel, inverse = load_products(
        *(
            pltpu.with_memory_space_constraint(whole, pltpu.HBM)
            for whole in (trace, double_layer[0, 0], single_inverse[0, 0], interface, node_mode[0])
        ),
        mode_weight[0],
    )
    near = swap(coarse_inverse, "sub", 1)
    packed, near = lax.optimization_barrier((packed, near))
    matrices = [coarse_inverse, near, onward(near, "sub")]
    rows = exchange(packed, face)
    state, own, coarse, wide, coupling = trace, None, None, None, None
    for iteration in range(ITERS):
        last = iteration == ITERS - 1
        residual, rhs, *own = update(
            place, rows, flux, load, selector_t, basis, coarse, wide, coupling, subs if last else 1
        )
        own = own[0] if own else None
        if last:
            residual, before = settle(state, residual, tall, own)
            gathered = lax.all_to_all(rhs, "sub", 0, 0, tiled=True)
            gathered, before = lax.optimization_barrier((gathered, before))
            gathered = gathered.reshape(subs, MODES, width)
            product = coarse_product(jnp.zeros_like(row_place), gathered, matrices[:1])
            final = share_of_sum(product[0])
            break
        got = swap(rhs, "sub", 1)
        pieces = jnp.stack([rhs, got])
        state, flux, packed = products(state, residual, kernel, inverse, selector, tall, own)
        pieces, packed, matrices = lax.optimization_barrier((pieces, packed, matrices))
        rows = exchange(packed, face)
        if iteration == 0:
            wide, wide_rows = flux[:, width:], rows[:, :, width:]
            flux, rows = flux[:, :width], rows[:, :, :width]
            coupling = couple(selector_t, wide, wide_rows)
        while pieces.shape[0] < subs:
            got = swap(pieces, "sub", pieces.shape[0])
            pieces = jnp.concatenate([pieces, got])
        coarse = sum_over_columns(coarse_product(row_place, pieces, matrices))
    trace = finish(before, tall, final)
    return trace[None, None], residual[None, None]


def solution(mesh):
    placed = (
        P("sub", "col", None, None),
        P("sub", "col", None, None),
        P("sub", "col", None, None),
        P("sub", "col", None, None),
        P("sub", "col", None, None),
        P("sub", "col", None),
        P("sub", "col", None),
        P("sub", "col"),
    )
    return jax.shard_map(
        local,
        mesh=mesh,
        in_specs=placed,
        out_specs=(P("sub", "col", None, None), P("sub", "col", None, None)),
        check_vma=False,
    )
```

```python
import functools

import jax
import jax.numpy as jnp
from jax import lax
from jax.experimental import pallas as pl
from jax.experimental.pallas import tpu as pltpu
from jax.sharding import PartitionSpec as P

MODES = 64
ITERS = 3
LANES = 128

bf16 = jnp.bfloat16
f32 = jnp.float32
DIRECTIONS = ((-1, -1), (-1, 0), (-1, 1), (0, -1), (0, 1), (1, -1), (1, 0), (1, 1))
PACKED = ((4, 1), (2, 0), (7, 0), (3, 1), (0, 0), (5, 0), (6, 1), (1, 1))

vmem = pl.BlockSpec(memory_space=pltpu.VMEM)
smem = pl.BlockSpec(memory_space=pltpu.SMEM)
hbm = pl.BlockSpec(memory_space=pl.ANY)
shape_of = jax.ShapeDtypeStruct
params = pltpu.CompilerParams(vmem_limit_bytes=16 * 1024 * 1024)
large = pltpu.CompilerParams(vmem_limit_bytes=16 * 1024 * 1024)


def dot(a, b):
    return jnp.dot(a, b, preferred_element_type=f32)


def pick(face, sel_ref, flux_ref, packed_ref):
    at = 0
    for d, whole in PACKED:
        size = face if whole else face // 8
        rows = dot(sel_ref[d, :size, :], flux_ref[d * face : (d + 1) * face, :])
        packed_ref[at : at + size, :] = rows.astype(bf16)
        at += size


def load_kernel(face, chunk, ahead, u_hbm, k_hbm, s_hbm, nodes_hbm, mode_hbm, weight_ref, flux_ref, packed_ref, sel_ref, selt_ref, basis_ref, tall_ref, k_ref, s_ref, mixed, u_ref, nodes_ref, mode_ref, sems, small_sems):
    count = u_ref.shape[0] // chunk
    small = ((u_hbm, u_ref), (nodes_hbm, nodes_ref), (mode_hbm, mode_ref))
    small = [pltpu.make_async_copy(*pair, small_sems.at[i]) for i, pair in enumerate(small)]
    for copy in small:
        copy.start()
    copies = []
    for which, (source, target) in enumerate(((k_hbm, k_ref), (s_hbm, s_ref))):
        for i in range(count):
            rows = pl.ds(i * chunk, chunk)
            copies.append(pltpu.make_async_copy(source.at[rows], target.at[rows], sems.at[which, i]))
    for copy in copies[:ahead]:
        copy.start()
    modes = basis_ref.shape[0]
    slot = lax.broadcasted_iota(jnp.int32, (face, face), 0)
    mode = lax.broadcasted_iota(jnp.int32, (modes, LANES), 0)
    blocks = u_ref.shape[0] // LANES

    def prepare(step, steps):
        for d in range(8 * step // steps, 8 * (step + 1) // steps):
            chosen = (slot == nodes_ref[d : d + 1, :] - d * face).astype(f32)
            selt_ref[d] = chosen.astype(bf16)
            sel_ref[d] = chosen.T.astype(bf16)
        for i in range(blocks * step // steps, blocks * (step + 1) // steps):
            rows = pl.ds(i * LANES, LANES)
            part = jnp.where(mode == mode_ref[:, rows], weight_ref[:, rows].astype(f32), 0.0)
            basis_ref[:, rows] = part.astype(bf16)
            tall_ref[rows, :] = jnp.concatenate([part] * (LANES // modes)).T.astype(bf16)

    for copy in small:
        copy.wait()
    u = u_ref[...]
    for i in range(2 * count):
        prepare(i, 2 * count)
        copies[i].wait()
        if i + ahead < 2 * count:
            copies[i + ahead].start()
        rows = pl.ds(i % count * chunk, chunk)
        if i < count:
            mixed[rows, :] = (0.5 * u_ref[rows, :].astype(f32) + dot(k_ref[rows, :], u)).astype(bf16)
        else:
            flux_ref[rows, :] = dot(s_ref[rows, :], mixed[...]).astype(bf16)
    pick(face, sel_ref, flux_ref, packed_ref)


def load_products(trace, kernel, inverse, nodes, mode, weight):
    count, width = trace.shape
    face = nodes.shape[1]
    chunk = 256 if count % 256 == 0 else count
    return pl.pallas_call(
        functools.partial(load_kernel, face, chunk, 3),
        out_shape=[
            shape_of((count, width), bf16),
            shape_of((4 * (face + face // 8), width), bf16),
            shape_of((8, face, face), bf16),
            shape_of((8, face, face), bf16),
            shape_of((MODES, count), bf16),
            shape_of((count, LANES), bf16),
            pltpu.VMEM((count, count), bf16),
            pltpu.VMEM((count, count), bf16),
        ],
        in_specs=[hbm] * 5 + [vmem],
        out_specs=[vmem] * 8,
        scratch_shapes=[
            pltpu.VMEM((count, width), bf16),
            pltpu.VMEM((count, width), bf16),
            pltpu.VMEM(nodes.shape, jnp.int32),
            pltpu.VMEM(mode.shape, jnp.int32),
            pltpu.SemaphoreType.DMA((2, count // chunk)),
            pltpu.SemaphoreType.DMA((3,)),
        ],
        compiler_params=large,
        cost_estimate=pl.CostEstimate(
            flops=4 * count * count * 2 * LANES, bytes_accessed=4 * count * count, transcendentals=0
        ),
        name="load_products",
    )(trace, kernel, inverse, nodes, mode, weight)


def products_kernel(face, chunk, state_ref, res_ref, k_ref, s_ref, sel_ref, tall_ref, c_ref, u_ref, flux_ref, packed_ref, entering, mixed):
    count, width = u_ref.shape
    for i in range(count // chunk):
        rows = pl.ds(i * chunk, chunk)
        following = state_ref[rows, :].astype(f32) + 0.25 * res_ref[rows, :].astype(f32)
        if c_ref is not None:
            following += dot(tall_ref[rows, : c_ref.shape[0]], c_ref[...])
        u_ref[rows, :] = following.astype(bf16)
        entering[rows, :width] = following.astype(bf16)
        if c_ref is None:
            entering[rows, width:] = tall_ref[rows, :]
    u = entering[...]
    for i in range(count // chunk):
        rows = pl.ds(i * chunk, chunk)
        mixed[rows, :] = (0.5 * entering[rows, :].astype(f32) + dot(k_ref[rows, :], u)).astype(bf16)
    m = mixed[...]
    for i in range(count // chunk):
        rows = pl.ds(i * chunk, chunk)
        flux_ref[rows, :] = dot(s_ref[rows, :], m).astype(bf16)
    pick(face, sel_ref, flux_ref, packed_ref)


def products(state, residual, kernel, inverse, selector, tall, own):
    count, width = state.shape
    face = selector.shape[1]
    chunk = 256 if count % 256 == 0 else count
    wide = width + LANES if own is None else width
    operands = [state, residual, kernel, inverse, selector, tall]
    body = functools.partial(products_kernel, face, chunk)
    if own is None:
        inner = body
        body = lambda *refs: inner(*refs[:6], None, *refs[6:])
    else:
        operands.append(own)
    return pl.pallas_call(
        body,
        out_shape=[
            shape_of((count, width), bf16),
            shape_of((count, wide), bf16),
            shape_of((4 * (face + face // 8), wide), bf16),
        ],
        in_specs=[vmem] * len(operands),
        out_specs=[vmem] * 3,
        scratch_shapes=[pltpu.VMEM((count, wide), bf16), pltpu.VMEM((count, wide), bf16)],
        compiler_params=params,
        cost_estimate=pl.CostEstimate(
            flops=4 * count * count * 2 * LANES, bytes_accessed=4 * count * count, transcendentals=0
        ),
        name="products",
    )(*operands)


def arrivals(face):
    corner = face // 8
    found = {4: (0, 0), 3: (1, 0), 6: (2, 0), 1: (3, 0)}
    found |= {7: (2, face), 5: (2, face + corner), 2: (3, face), 0: (3, face + corner)}
    return [found[d] + (face if d in (1, 3, 4, 6) else corner,) for d in range(8)]


def couple_kernel(modes, selt_ref, w_ref, wrows_ref, out_ref):
    face = selt_ref.shape[1]
    lane = lax.broadcasted_iota(jnp.int32, (face, LANES), 1)
    for d, (group, at, size) in enumerate(arrivals(face)):
        theirs = dot(selt_ref[d, :, :size], wrows_ref[group, at : at + size, :])
        mine = w_ref[d * face : (d + 1) * face, :].astype(f32)
        out_ref[d, :, :face] = selt_ref[d]
        out_ref[d, :, face:] = jnp.where(lane < modes, theirs, mine).astype(bf16)


def couple(selector_t, wide, wide_rows):
    face = selector_t.shape[1]
    return pl.pallas_call(
        functools.partial(couple_kernel, MODES),
        out_shape=shape_of((8, face, face + LANES), bf16),
        in_specs=[vmem] * 3,
        out_specs=vmem,
        compiler_params=params,
        name="couple",
    )(selector_t, wide, wide_rows)


def first_update_kernel(rows_ref, flux_ref, load_ref, selt_ref, basis_ref, res_ref, rhs_ref):
    face = selt_ref.shape[1]
    for d, (group, at, size) in enumerate(arrivals(face)):
        band = slice(d * face, (d + 1) * face)
        placed = dot(selt_ref[d, :, :size], rows_ref[group, at : at + size, :])
        assembled = flux_ref[band, :].astype(f32) + placed
        res_ref[band, :] = (load_ref[band, :].astype(f32) - assembled).astype(bf16)
    rest = slice(8 * face, None)
    res_ref[rest, :] = (load_ref[rest, :].astype(f32) - flux_ref[rest, :].astype(f32)).astype(bf16)
    rhs_ref[...] = dot(basis_ref[...], res_ref[...]).astype(bf16)


def update_kernel(half, row_ref, col_ref, rows_ref, flux_ref, load_ref, couple_ref, basis_ref, c_ref, w_ref, res_ref, rhs_ref, own_ref, right):
    face = couple_ref.shape[1]
    modes = basis_ref.shape[0]
    odd, col = row_ref[0] % 2, col_ref[0]
    base = col // half * (half - 1)

    def results(row_step, col_step):
        source = (0, 1 + odd, 2 - odd)[row_step]
        beside = jnp.clip(col + col_step, base, base + half) - base
        return c_ref[source, pl.ds(pl.multiple_of(beside * modes, modes), modes), :]

    own = results(0, 0)
    own_ref[...] = own
    for d, (group, at, size) in enumerate(arrivals(face)):
        band = slice(d * face, (d + 1) * face)
        right[d, :size, :] = rows_ref[group, at : at + size, :]
        if size < face:
            right[d, size:face, :] = jnp.zeros((face - size, right.shape[2]), bf16)
        right[d, face : face + modes, :] = results(*DIRECTIONS[d])
        right[d, face + modes :, :] = own
        assembled = flux_ref[band, :].astype(f32) + dot(couple_ref[d], right[d])
        res_ref[band, :] = (load_ref[band, :].astype(f32) - assembled).astype(bf16)
    rest = slice(8 * face, None)
    assembled = flux_ref[rest, :].astype(f32) + dot(w_ref[rest, :modes], own)
    res_ref[rest, :] = (load_ref[rest, :].astype(f32) - assembled).astype(bf16)
    rhs = dot(basis_ref[...], res_ref[...]).astype(bf16)
    for i in range(rhs_ref.shape[0] // modes):
        rhs_ref[i * modes : (i + 1) * modes, :] = rhs


def settle_kernel(chunk, state_ref, res_ref, tall_ref, own_ref, out_hbm, before_ref, sem):
    copy = pltpu.make_async_copy(res_ref, out_hbm, sem)
    copy.start()
    for i in range(state_ref.shape[0] // chunk):
        rows = pl.ds(i * chunk, chunk)
        product = dot(tall_ref[rows, : own_ref.shape[0]], own_ref[...])
        gained = state_ref[rows, :].astype(f32) + 0.25 * res_ref[rows, :].astype(f32)
        before_ref[rows, :] = gained + product
    copy.wait()


def settle(state, residual, tall, own):
    count = state.shape[0]
    return pl.pallas_call(
        functools.partial(settle_kernel, 256 if count % 256 == 0 else count),
        out_shape=[shape_of(state.shape, bf16), shape_of(state.shape, f32)],
        in_specs=[vmem] * 4,
        out_specs=[hbm, vmem],
        scratch_shapes=[pltpu.SemaphoreType.DMA],
        compiler_params=params,
        name="settle",
    )(state, residual, tall, own)


def finish_kernel(chunk, before_ref, tall_ref, own_ref, trace_hbm, trace, sems):
    copies = []
    for i in range(before_ref.shape[0] // chunk):
        rows = pl.ds(i * chunk, chunk)
        product = dot(tall_ref[rows, : own_ref.shape[0]], own_ref[...])
        trace[rows, :] = (before_ref[rows, :] + product).astype(bf16)
        copies.append(pltpu.make_async_copy(trace.at[rows], trace_hbm.at[rows], sems.at[i]))
        copies[-1].start()
    for copy in copies:
        copy.wait()


def finish(before, tall, own):
    count = before.shape[0]
    chunk = 256 if count % 256 == 0 else count
    return pl.pallas_call(
        functools.partial(finish_kernel, chunk),
        out_shape=shape_of(before.shape, bf16),
        in_specs=[vmem] * 3,
        out_specs=hbm,
        scratch_shapes=[
            pltpu.VMEM(before.shape, bf16),
            pltpu.SemaphoreType.DMA((count // chunk,)),
        ],
        compiler_params=params,
        name="finish",
    )(before, tall, own)


def update(place, half, rows, flux, load, selector_t, basis, coarse, wide, coupling, copies=1):
    count, width = load.shape
    modes = basis.shape[0]
    face = selector_t.shape[1]
    outs = [shape_of((count, width), bf16), shape_of((copies * modes, width), bf16)]
    if coarse is None:
        operands = [rows, flux, load, selector_t, basis]
        return pl.pallas_call(
            first_update_kernel,
            out_shape=outs,
            in_specs=[vmem] * 5,
            out_specs=[vmem] * 2,
            compiler_params=params,
            name="first_update",
        )(*operands)
    operands = [*place, rows, flux, load, coupling, basis, coarse, wide]
    return pl.pallas_call(
        functools.partial(update_kernel, half),
        out_shape=outs + [shape_of((modes, width), bf16)],
        in_specs=[smem] * 2 + [vmem] * 7,
        out_specs=[vmem] * 3,
        scratch_shapes=[pltpu.VMEM((8, face + LANES, width), bf16)],
        compiler_params=params,
        name="update",
    )(*operands)


def coarse_kernel(modes, half, ordered, row_ref, col_ref, pieces_ref, *refs):
    matrices, (mine_ref, sent_ref, full, whole) = refs[:-4], refs[-4:]
    for m in range(pieces_ref.shape[0]):
        block = m if ordered else row_ref[0] ^ m
        full[pl.ds(pl.multiple_of(block * modes, modes), modes), :] = pieces_ref[m]
    count = mine_ref.shape[1]
    upper = col_ref[0] // half
    mine = pl.multiple_of(upper * (2 * half * modes - count), modes)
    sent = pl.multiple_of((1 - upper) * (2 * half * modes - count), modes)
    for i, matrix in enumerate(matrices):
        whole[i] = dot(matrix[...], full[...])
        mine_ref[i] = whole[i, pl.ds(mine, count), :]
        sent_ref[i] = whole[i, pl.ds(sent, count), :].astype(bf16)


def coarse_product(place, half, pieces, matrices, count, ordered=False):
    many, modes, width = pieces.shape
    rows, depth = matrices[0].shape
    return pl.pallas_call(
        functools.partial(coarse_kernel, modes, half, ordered),
        out_shape=[
            shape_of((len(matrices), count, width), f32),
            shape_of((len(matrices), count, width), bf16),
        ],
        in_specs=[smem] * 2 + [vmem] * (1 + len(matrices)),
        out_specs=[vmem] * 2,
        scratch_shapes=[
            pltpu.VMEM((depth, width), bf16),
            pltpu.VMEM((len(matrices), rows, width), f32),
        ],
        compiler_params=params,
        cost_estimate=pl.CostEstimate(
            flops=2 * len(matrices) * rows * depth * width,
            bytes_accessed=2 * len(matrices) * rows * depth,
            transcendentals=0,
        ),
        name="coarse_product",
    )(*place, pieces, *matrices)


def swap(value, axis, mask):
    return lax.ppermute(value, axis, [(i, i ^ mask) for i in range(lax.axis_size(axis))])


def cross(value, axis):
    subs, cols = lax.axis_size("sub"), lax.axis_size("col")
    pairs = []
    for sub in range(subs):
        for col in range(cols):
            to = [sub, col]
            k = 0 if axis == "sub" else 1
            n = (subs, cols)[k]
            near = to[k] + 1 if to[k] % 2 else to[k] - 1
            if 0 <= near < n or n <= 4:
                to[k] = near % n
            else:
                to[1 - k] ^= 1
            pairs.append((sub * cols + col, to[0] * cols + to[1]))
    return lax.ppermute(value, ("sub", "col"), pairs)


def onward(value, axis):
    n = lax.axis_size(axis)
    ring = list(range(0, n, 2)) + list(range(n - 1, 0, -2))
    return lax.ppermute(value, axis, [(ring[i - 1], ring[i]) for i in range(n)])


def trade(forward, backward, axis):
    even = lax.axis_index(axis) % 2 == 0
    near = swap(jnp.where(even, forward, backward), axis, 1)
    far = cross(jnp.where(even, backward, forward), axis)
    return jnp.where(even, near, far), jnp.where(even, far, near)


def exchange(packed, face):
    corner = face // 8
    group = face + 2 * corner
    right, left = trade(packed[:group], packed[group : 2 * group], "col")
    six, one = packed[2 * group : 2 * group + face], packed[2 * group + face :]
    up = jnp.concatenate([six, right[face + corner :], left[face + corner :]])
    down = jnp.concatenate([one, right[face : face + corner], left[face : face + corner]])
    above, below = trade(up, down, "sub")
    return jnp.stack([right, left, above, below])


def sum_over_columns(value, sent):
    bit = lax.axis_size("col") // 2
    while bit:
        value = value + swap(sent, "col", bit).astype(f32)
        sent = value.astype(bf16)
        bit //= 2
    return sent


def share_of_sum(value, sent):
    bit = lax.axis_size("col") // 2
    while True:
        value = value + swap(sent, "col", bit | 1).astype(f32)
        bit //= 2
        if not bit:
            return value.astype(bf16)
        half = value.shape[0] // 2
        upper = (lax.axis_index("col") // bit) % 2 == 1
        low, high = value[:half], value[half:]
        sent = jnp.where(upper, low, high).astype(bf16)
        value = jnp.where(upper, high, low)


def local(
    trace_start,
    neumann_load,
    double_layer,
    single_inverse,
    interface_nodes,
    node_mode,
    mode_weight,
    coarse_inverse,
):
    subs, cols = lax.axis_size("sub"), lax.axis_size("col")
    row, col = lax.axis_index("sub"), lax.axis_index("col")
    trace = trace_start[0, 0]
    load = neumann_load[0, 0]
    width = trace.shape[1]
    interface = interface_nodes[0, 0]
    face = interface.shape[1]

    half = cols // 2
    place = [jnp.reshape(index, (1,)).astype(jnp.int32) for index in (row, col)]
    trace, place = lax.optimization_barrier((trace, place))

    flux, packed, selector, selector_t, basis, tall, kernel, inverse = load_products(
        *(
            pltpu.with_memory_space_constraint(whole, pltpu.HBM)
            for whole in (trace, double_layer[0, 0], single_inverse[0, 0], interface, node_mode[0])
        ),
        mode_weight[0],
    )
    near = swap(coarse_inverse, "sub", 1)
    packed, near = lax.optimization_barrier((packed, near))
    matrices = [coarse_inverse, near, onward(near, "sub")]
    rows = exchange(packed, face)
    state, own, coarse, wide, coupling = trace, None, None, None, None
    for iteration in range(ITERS):
        last = iteration == ITERS - 1
        residual, rhs, *own = update(
            place, half, rows, flux, load, selector_t, basis, coarse, wide, coupling, subs if last else 1
        )
        own = own[0] if own else None
        if last:
            residual, before = settle(state, residual, tall, own)
            gathered = lax.all_to_all(rhs, "sub", 0, 0, tiled=True)
            gathered, before = lax.optimization_barrier((gathered, before))
            gathered = gathered.reshape(subs, MODES, width)
            value, sent = coarse_product(
                place, half, gathered, matrices[:1], half * MODES, ordered=True
            )
            final = share_of_sum(value[0], sent[0])
            break
        got = swap(rhs, "sub", 1)
        pieces = jnp.stack([rhs, got])
        state, flux, packed = products(state, residual, kernel, inverse, selector, tall, own)
        pieces, packed, matrices = lax.optimization_barrier((pieces, packed, matrices))
        rows = exchange(packed, face)
        if iteration == 0:
            wide, wide_rows = flux[:, width:], rows[:, :, width:]
            flux, rows = flux[:, :width], rows[:, :, :width]
            coupling = couple(selector_t, wide, wide_rows)
        while pieces.shape[0] < subs:
            got = swap(pieces, "sub", pieces.shape[0])
            pieces = jnp.concatenate([pieces, got])
        coarse = sum_over_columns(*coarse_product(place, half, pieces, matrices, (half + 1) * MODES))
    trace = finish(before, tall, final)
    return trace[None, None], residual[None, None]


def solution(mesh):
    placed = (
        P("sub", "col", None, None),
        P("sub", "col", None, None),
        P("sub", "col", None, None),
        P("sub", "col", None, None),
        P("sub", "col", None, None),
        P("sub", "col", None),
        P("sub", "col", None),
        P("sub", "col"),
    )
    return jax.shard_map(
        local,
        mesh=mesh,
        in_specs=placed,
        out_specs=(P("sub", "col", None, None), P("sub", "col", None, None)),
        check_vma=False,
    )
```

```python
import functools

import jax
import jax.numpy as jnp
from jax import lax
from jax.experimental import pallas as pl
from jax.experimental.pallas import tpu as pltpu
from jax.sharding import PartitionSpec as P

MODES = 64
ITERS = 3
LANES = 128

bf16 = jnp.bfloat16
f32 = jnp.float32
DIRECTIONS = ((-1, -1), (-1, 0), (-1, 1), (0, -1), (0, 1), (1, -1), (1, 0), (1, 1))
PACKED = ((4, 1), (2, 0), (7, 0), (3, 1), (0, 0), (5, 0), (6, 1), (1, 1))

vmem = pl.BlockSpec(memory_space=pltpu.VMEM)
smem = pl.BlockSpec(memory_space=pltpu.SMEM)
hbm = pl.BlockSpec(memory_space=pl.ANY)
shape_of = jax.ShapeDtypeStruct
params = pltpu.CompilerParams(vmem_limit_bytes=16 * 1024 * 1024)
large = pltpu.CompilerParams(vmem_limit_bytes=16 * 1024 * 1024)


def dot(a, b):
    return jnp.dot(a, b, preferred_element_type=f32)


def pick(face, sel_ref, flux_ref, packed_ref):
    at = 0
    for d, whole in PACKED:
        size = face if whole else face // 8
        rows = dot(sel_ref[d, :size, :], flux_ref[d * face : (d + 1) * face, :])
        packed_ref[at : at + size, :] = rows.astype(bf16)
        at += size


def load_kernel(face, chunk, ahead, u_hbm, k_hbm, s_hbm, nodes_hbm, mode_hbm, weight_ref, flux_ref, packed_ref, sel_ref, selt_ref, basis_ref, tall_ref, k_ref, s_ref, mixed, u_ref, nodes_ref, mode_ref, sems, small_sems):
    count = u_ref.shape[0] // chunk
    small = ((u_hbm, u_ref), (nodes_hbm, nodes_ref), (mode_hbm, mode_ref))
    small = [pltpu.make_async_copy(*pair, small_sems.at[i]) for i, pair in enumerate(small)]
    for copy in small:
        copy.start()
    copies = []
    for which, (source, target) in enumerate(((k_hbm, k_ref), (s_hbm, s_ref))):
        for i in range(count):
            rows = pl.ds(i * chunk, chunk)
            copies.append(pltpu.make_async_copy(source.at[rows], target.at[rows], sems.at[which, i]))
    for copy in copies[:ahead]:
        copy.start()
    modes = basis_ref.shape[0]
    slot = lax.broadcasted_iota(jnp.int32, (face, face), 0)
    mode = lax.broadcasted_iota(jnp.int32, (modes, LANES), 0)
    blocks = u_ref.shape[0] // LANES

    def prepare(step, steps):
        for d in range(8 * step // steps, 8 * (step + 1) // steps):
            chosen = (slot == nodes_ref[d : d + 1, :] - d * face).astype(f32)
            selt_ref[d] = chosen.astype(bf16)
            sel_ref[d] = chosen.T.astype(bf16)
        for i in range(blocks * step // steps, blocks * (step + 1) // steps):
            rows = pl.ds(i * LANES, LANES)
            part = jnp.where(mode == mode_ref[:, rows], weight_ref[:, rows].astype(f32), 0.0)
            basis_ref[:, rows] = part.astype(bf16)
            tall_ref[rows, :] = jnp.concatenate([part] * (LANES // modes)).T.astype(bf16)

    for copy in small:
        copy.wait()
    u = u_ref[...]
    for i in range(2 * count):
        prepare(i, 2 * count)
        copies[i].wait()
        if i + ahead < 2 * count:
            copies[i + ahead].start()
        rows = pl.ds(i % count * chunk, chunk)
        if i < count:
            mixed[rows, :] = (0.5 * u_ref[rows, :].astype(f32) + dot(k_ref[rows, :], u)).astype(bf16)
        else:
            flux_ref[rows, :] = dot(s_ref[rows, :], mixed[...]).astype(bf16)
    pick(face, sel_ref, flux_ref, packed_ref)


def load_products(trace, kernel, inverse, nodes, mode, weight):
    count, width = trace.shape
    face = nodes.shape[1]
    chunk = 256 if count % 256 == 0 else count
    return pl.pallas_call(
        functools.partial(load_kernel, face, chunk, 3),
        out_shape=[
            shape_of((count, width), bf16),
            shape_of((4 * (face + face // 8), width), bf16),
            shape_of((8, face, face), bf16),
            shape_of((8, face, face), bf16),
            shape_of((MODES, count), bf16),
            shape_of((count, LANES), bf16),
            pltpu.VMEM((count, count), bf16),
            pltpu.VMEM((count, count), bf16),
        ],
        in_specs=[hbm] * 5 + [vmem],
        out_specs=[vmem] * 8,
        scratch_shapes=[
            pltpu.VMEM((count, width), bf16),
            pltpu.VMEM((count, width), bf16),
            pltpu.VMEM(nodes.shape, jnp.int32),
            pltpu.VMEM(mode.shape, jnp.int32),
            pltpu.SemaphoreType.DMA((2, count // chunk)),
            pltpu.SemaphoreType.DMA((3,)),
        ],
        compiler_params=large,
        cost_estimate=pl.CostEstimate(
            flops=4 * count * count * 2 * LANES, bytes_accessed=4 * count * count, transcendentals=0
        ),
        name="load_products",
    )(trace, kernel, inverse, nodes, mode, weight)


def products_kernel(face, chunk, state_ref, res_ref, k_ref, s_ref, sel_ref, tall_ref, c_ref, u_ref, flux_ref, packed_ref, entering, mixed):
    count, width = u_ref.shape
    for i in range(count // chunk):
        rows = pl.ds(i * chunk, chunk)
        following = state_ref[rows, :].astype(f32) + 0.25 * res_ref[rows, :].astype(f32)
        if c_ref is not None:
            following += dot(tall_ref[rows, : c_ref.shape[0]], c_ref[...])
        u_ref[rows, :] = following.astype(bf16)
        entering[rows, :width] = following.astype(bf16)
        if c_ref is None:
            entering[rows, width:] = tall_ref[rows, :]
    u = entering[...]
    for i in range(count // chunk):
        rows = pl.ds(i * chunk, chunk)
        mixed[rows, :] = (0.5 * entering[rows, :].astype(f32) + dot(k_ref[rows, :], u)).astype(bf16)
    m = mixed[...]
    for i in range(count // chunk):
        rows = pl.ds(i * chunk, chunk)
        flux_ref[rows, :] = dot(s_ref[rows, :], m).astype(bf16)
    pick(face, sel_ref, flux_ref, packed_ref)


def products(state, residual, kernel, inverse, selector, tall, own):
    count, width = state.shape
    face = selector.shape[1]
    chunk = 256 if count % 256 == 0 else count
    wide = width + LANES if own is None else width
    operands = [state, residual, kernel, inverse, selector, tall]
    body = functools.partial(products_kernel, face, chunk)
    if own is None:
        inner = body
        body = lambda *refs: inner(*refs[:6], None, *refs[6:])
    else:
        operands.append(own)
    return pl.pallas_call(
        body,
        out_shape=[
            shape_of((count, width), bf16),
            shape_of((count, wide), bf16),
            shape_of((4 * (face + face // 8), wide), bf16),
        ],
        in_specs=[vmem] * len(operands),
        out_specs=[vmem] * 3,
        scratch_shapes=[pltpu.VMEM((count, wide), bf16), pltpu.VMEM((count, wide), bf16)],
        compiler_params=params,
        cost_estimate=pl.CostEstimate(
            flops=4 * count * count * 2 * LANES, bytes_accessed=4 * count * count, transcendentals=0
        ),
        name="products",
    )(*operands)


def arrivals(face):
    corner = face // 8
    found = {4: (0, 0), 3: (1, 0), 6: (2, 0), 1: (3, 0)}
    found |= {7: (2, face), 5: (2, face + corner), 2: (3, face), 0: (3, face + corner)}
    return [found[d] + (face if d in (1, 3, 4, 6) else corner,) for d in range(8)]


def couple_kernel(modes, selt_ref, w_ref, wrows_ref, out_ref):
    face = selt_ref.shape[1]
    lane = lax.broadcasted_iota(jnp.int32, (face, LANES), 1)
    for d, (group, at, size) in enumerate(arrivals(face)):
        theirs = dot(selt_ref[d, :, :size], wrows_ref[group, at : at + size, :])
        mine = w_ref[d * face : (d + 1) * face, :].astype(f32)
        out_ref[d, :, :face] = selt_ref[d]
        out_ref[d, :, face:] = jnp.where(lane < modes, theirs, mine).astype(bf16)


def couple(selector_t, wide, wide_rows):
    face = selector_t.shape[1]
    return pl.pallas_call(
        functools.partial(couple_kernel, MODES),
        out_shape=shape_of((8, face, face + LANES), bf16),
        in_specs=[vmem] * 3,
        out_specs=vmem,
        compiler_params=params,
        name="couple",
    )(selector_t, wide, wide_rows)


def first_update_kernel(rows_ref, flux_ref, load_ref, selt_ref, basis_ref, res_ref, rhs_ref):
    face = selt_ref.shape[1]
    for d, (group, at, size) in enumerate(arrivals(face)):
        band = slice(d * face, (d + 1) * face)
        placed = dot(selt_ref[d, :, :size], rows_ref[group, at : at + size, :])
        assembled = flux_ref[band, :].astype(f32) + placed
        res_ref[band, :] = (load_ref[band, :].astype(f32) - assembled).astype(bf16)
    rest = slice(8 * face, None)
    res_ref[rest, :] = (load_ref[rest, :].astype(f32) - flux_ref[rest, :].astype(f32)).astype(bf16)
    rhs_ref[...] = dot(basis_ref[...], res_ref[...]).astype(bf16)


def update_kernel(half, row_ref, col_ref, rows_ref, flux_ref, load_ref, couple_ref, basis_ref, c_ref, w_ref, res_ref, rhs_ref, own_ref, right):
    face = couple_ref.shape[1]
    modes = basis_ref.shape[0]
    odd, col = row_ref[0] % 2, col_ref[0]
    base = col // half * (half - 1)

    def results(row_step, col_step):
        source = (0, 1 + odd, 2 - odd)[row_step]
        beside = jnp.clip(col + col_step, base, base + half) - base
        return c_ref[source, pl.ds(pl.multiple_of(beside * modes, modes), modes), :]

    own = results(0, 0)
    own_ref[...] = own
    for d, (group, at, size) in enumerate(arrivals(face)):
        band = slice(d * face, (d + 1) * face)
        right[d, :size, :] = rows_ref[group, at : at + size, :]
        if size < face:
            right[d, size:face, :] = jnp.zeros((face - size, right.shape[2]), bf16)
        right[d, face : face + modes, :] = results(*DIRECTIONS[d])
        right[d, face + modes :, :] = own
        assembled = flux_ref[band, :].astype(f32) + dot(couple_ref[d], right[d])
        res_ref[band, :] = (load_ref[band, :].astype(f32) - assembled).astype(bf16)
    rest = slice(8 * face, None)
    assembled = flux_ref[rest, :].astype(f32) + dot(w_ref[rest, :modes], own)
    res_ref[rest, :] = (load_ref[rest, :].astype(f32) - assembled).astype(bf16)
    rhs = dot(basis_ref[...], res_ref[...]).astype(bf16)
    for i in range(rhs_ref.shape[0] // modes):
        rhs_ref[i * modes : (i + 1) * modes, :] = rhs


def settle_kernel(chunk, state_ref, res_ref, tall_ref, own_ref, out_hbm, before_ref, sem):
    copy = pltpu.make_async_copy(res_ref, out_hbm, sem)
    copy.start()
    for i in range(state_ref.shape[0] // chunk):
        rows = pl.ds(i * chunk, chunk)
        product = dot(tall_ref[rows, : own_ref.shape[0]], own_ref[...])
        gained = state_ref[rows, :].astype(f32) + 0.25 * res_ref[rows, :].astype(f32)
        before_ref[rows, :] = gained + product
    copy.wait()


def settle(state, residual, tall, own):
    count = state.shape[0]
    return pl.pallas_call(
        functools.partial(settle_kernel, 256 if count % 256 == 0 else count),
        out_shape=[shape_of(state.shape, bf16), shape_of(state.shape, f32)],
        in_specs=[vmem] * 4,
        out_specs=[hbm, vmem],
        scratch_shapes=[pltpu.SemaphoreType.DMA],
        compiler_params=params,
        name="settle",
    )(state, residual, tall, own)


def finish_kernel(chunk, before_ref, tall_ref, own_ref, trace_hbm, trace, sems):
    copies = []
    for i in range(before_ref.shape[0] // chunk):
        rows = pl.ds(i * chunk, chunk)
        product = dot(tall_ref[rows, : own_ref.shape[0]], own_ref[...])
        trace[rows, :] = (before_ref[rows, :] + product).astype(bf16)
        copies.append(pltpu.make_async_copy(trace.at[rows], trace_hbm.at[rows], sems.at[i]))
        copies[-1].start()
    for copy in copies:
        copy.wait()


def finish(before, tall, own):
    count = before.shape[0]
    chunk = 256 if count % 256 == 0 else count
    return pl.pallas_call(
        functools.partial(finish_kernel, chunk),
        out_shape=shape_of(before.shape, bf16),
        in_specs=[vmem] * 3,
        out_specs=hbm,
        scratch_shapes=[
            pltpu.VMEM(before.shape, bf16),
            pltpu.SemaphoreType.DMA((count // chunk,)),
        ],
        compiler_params=params,
        name="finish",
    )(before, tall, own)


def update(place, half, rows, flux, load, selector_t, basis, coarse, wide, coupling, copies=1):
    count, width = load.shape
    modes = basis.shape[0]
    face = selector_t.shape[1]
    outs = [shape_of((count, width), bf16), shape_of((copies * modes, width), bf16)]
    if coarse is None:
        operands = [rows, flux, load, selector_t, basis]
        return pl.pallas_call(
            first_update_kernel,
            out_shape=outs,
            in_specs=[vmem] * 5,
            out_specs=[vmem] * 2,
            compiler_params=params,
            name="first_update",
        )(*operands)
    operands = [*place, rows, flux, load, coupling, basis, coarse, wide]
    return pl.pallas_call(
        functools.partial(update_kernel, half),
        out_shape=outs + [shape_of((modes, width), bf16)],
        in_specs=[smem] * 2 + [vmem] * 7,
        out_specs=[vmem] * 3,
        scratch_shapes=[pltpu.VMEM((8, face + LANES, width), bf16)],
        compiler_params=params,
        name="update",
    )(*operands)


def coarse_kernel(modes, half, order, row_ref, col_ref, pieces_ref, *refs):
    matrices, (mine_ref, sent_ref, full, whole) = refs[:-4], refs[-4:]
    for m in range(pieces_ref.shape[0]):
        block = row_ref[0] ^ order[m] if order else m
        full[pl.ds(pl.multiple_of(block * modes, modes), modes), :] = pieces_ref[m]
    count = mine_ref.shape[1]
    upper = col_ref[0] // half
    mine = pl.multiple_of(upper * (2 * half * modes - count), modes)
    sent = pl.multiple_of((1 - upper) * (2 * half * modes - count), modes)
    for i, matrix in enumerate(matrices):
        whole[i] = dot(matrix[...], full[...])
        mine_ref[i] = whole[i, pl.ds(mine, count), :]
        sent_ref[i] = whole[i, pl.ds(sent, count), :].astype(bf16)


def coarse_product(place, half, pieces, matrices, count, order=None):
    many, modes, width = pieces.shape
    rows, depth = matrices[0].shape
    return pl.pallas_call(
        functools.partial(coarse_kernel, modes, half, order),
        out_shape=[
            shape_of((len(matrices), count, width), f32),
            shape_of((len(matrices), count, width), bf16),
        ],
        in_specs=[smem] * 2 + [vmem] * (1 + len(matrices)),
        out_specs=[vmem] * 2,
        scratch_shapes=[
            pltpu.VMEM((depth, width), bf16),
            pltpu.VMEM((len(matrices), rows, width), f32),
        ],
        compiler_params=params,
        cost_estimate=pl.CostEstimate(
            flops=2 * len(matrices) * rows * depth * width,
            bytes_accessed=2 * len(matrices) * rows * depth,
            transcendentals=0,
        ),
        name="coarse_product",
    )(*place, pieces, *matrices)


def swap(value, axis, mask):
    return lax.ppermute(value, axis, [(i, i ^ mask) for i in range(lax.axis_size(axis))])


def cross(value, axis):
    subs, cols = lax.axis_size("sub"), lax.axis_size("col")
    pairs = []
    for sub in range(subs):
        for col in range(cols):
            to = [sub, col]
            k = 0 if axis == "sub" else 1
            n = (subs, cols)[k]
            near = to[k] + 1 if to[k] % 2 else to[k] - 1
            if 0 <= near < n or n <= 4:
                to[k] = near % n
            else:
                to[1 - k] ^= 1
            pairs.append((sub * cols + col, to[0] * cols + to[1]))
    return lax.ppermute(value, ("sub", "col"), pairs)


def onward(value, axis):
    n = lax.axis_size(axis)
    ring = list(range(0, n, 2)) + list(range(n - 1, 0, -2))
    return lax.ppermute(value, axis, [(ring[i - 1], ring[i]) for i in range(n)])


def trade(forward, backward, axis):
    even = lax.axis_index(axis) % 2 == 0
    near = swap(jnp.where(even, forward, backward), axis, 1)
    far = cross(jnp.where(even, backward, forward), axis)
    return jnp.where(even, near, far), jnp.where(even, far, near)


def exchange(packed, face):
    corner = face // 8
    group = face + 2 * corner
    right, left = trade(packed[:group], packed[group : 2 * group], "col")
    six, one = packed[2 * group : 2 * group + face], packed[2 * group + face :]
    up = jnp.concatenate([six, right[face + corner :], left[face + corner :]])
    down = jnp.concatenate([one, right[face : face + corner], left[face : face + corner]])
    above, below = trade(up, down, "sub")
    return jnp.stack([right, left, above, below])


def sum_over_columns(value, sent):
    bit = lax.axis_size("col") // 2
    while bit:
        value = value + swap(sent, "col", bit).astype(f32)
        sent = value.astype(bf16)
        bit //= 2
    return sent


def share_of_sum(value, sent):
    bit = lax.axis_size("col") // 2
    while True:
        value = value + swap(sent, "col", bit | 1).astype(f32)
        bit //= 2
        if not bit:
            return value.astype(bf16)
        half = value.shape[0] // 2
        upper = (lax.axis_index("col") // bit) % 2 == 1
        low, high = value[:half], value[half:]
        sent = jnp.where(upper, low, high).astype(bf16)
        value = jnp.where(upper, high, low)


def local(
    trace_start,
    neumann_load,
    double_layer,
    single_inverse,
    interface_nodes,
    node_mode,
    mode_weight,
    coarse_inverse,
):
    subs, cols = lax.axis_size("sub"), lax.axis_size("col")
    row, col = lax.axis_index("sub"), lax.axis_index("col")
    trace = trace_start[0, 0]
    load = neumann_load[0, 0]
    width = trace.shape[1]
    interface = interface_nodes[0, 0]
    face = interface.shape[1]

    half = cols // 2
    place = [jnp.reshape(index, (1,)).astype(jnp.int32) for index in (row, col)]
    trace, place = lax.optimization_barrier((trace, place))

    flux, packed, selector, selector_t, basis, tall, kernel, inverse = load_products(
        *(
            pltpu.with_memory_space_constraint(whole, pltpu.HBM)
            for whole in (trace, double_layer[0, 0], single_inverse[0, 0], interface, node_mode[0])
        ),
        mode_weight[0],
    )
    near = swap(coarse_inverse, "sub", 1)
    packed, near = lax.optimization_barrier((packed, near))
    matrices = [coarse_inverse, near, onward(near, "sub")]
    rows = exchange(packed, face)
    state, own, coarse, wide, coupling = trace, None, None, None, None
    for iteration in range(ITERS):
        last = iteration == ITERS - 1
        residual, rhs, *own = update(
            place, half, rows, flux, load, selector_t, basis, coarse, wide, coupling, subs if last else 1
        )
        own = own[0] if own else None
        if last:
            residual, before = settle(state, residual, tall, own)
            gathered = lax.all_to_all(rhs, "sub", 0, 0, tiled=True)
            gathered, before = lax.optimization_barrier((gathered, before))
            gathered = gathered.reshape(subs, MODES, width)
            value, sent = coarse_product(
                place, half, gathered, matrices[:1], half * MODES
            )
            final = share_of_sum(value[0], sent[0])
            break
        bits = [subs >> i for i in range(1, subs.bit_length())]
        order = [0, bits[0]]
        pieces = jnp.stack([rhs, swap(rhs, "sub", bits[0])])
        state, flux, packed = products(state, residual, kernel, inverse, selector, tall, own)
        pieces, packed, matrices = lax.optimization_barrier((pieces, packed, matrices))
        rows = exchange(packed, face)
        if iteration == 0:
            wide, wide_rows = flux[:, width:], rows[:, :, width:]
            flux, rows = flux[:, :width], rows[:, :, :width]
            coupling = couple(selector_t, wide, wide_rows)
        for bit in bits[1:]:
            order += [m ^ bit for m in order]
            pieces = jnp.concatenate([pieces, swap(pieces, "sub", bit)])
        coarse = sum_over_columns(*coarse_product(place, half, pieces, matrices, (half + 1) * MODES, order))
    trace = finish(before, tall, final)
    return trace[None, None], residual[None, None]


def solution(mesh):
    placed = (
        P("sub", "col", None, None),
        P("sub", "col", None, None),
        P("sub", "col", None, None),
        P("sub", "col", None, None),
        P("sub", "col", None, None),
        P("sub", "col", None),
        P("sub", "col", None),
        P("sub", "col"),
    )
    return jax.shard_map(
        local,
        mesh=mesh,
        in_specs=placed,
        out_specs=(P("sub", "col", None, None), P("sub", "col", None, None)),
        check_vma=False,
    )
```

```python
import functools

import jax
import jax.numpy as jnp
from jax import lax
from jax.experimental import pallas as pl
from jax.experimental.pallas import tpu as pltpu
from jax.sharding import PartitionSpec as P

MODES = 64
ITERS = 3
LANES = 128

bf16 = jnp.bfloat16
f32 = jnp.float32
DIRECTIONS = ((-1, -1), (-1, 0), (-1, 1), (0, -1), (0, 1), (1, -1), (1, 0), (1, 1))
PACKED = ((4, 1), (2, 0), (7, 0), (3, 1), (0, 0), (5, 0), (6, 1), (1, 1))

vmem = pl.BlockSpec(memory_space=pltpu.VMEM)
smem = pl.BlockSpec(memory_space=pltpu.SMEM)
hbm = pl.BlockSpec(memory_space=pl.ANY)
shape_of = jax.ShapeDtypeStruct
params = pltpu.CompilerParams(vmem_limit_bytes=16 * 1024 * 1024)


def dot(a, b):
    return jnp.dot(a, b, preferred_element_type=f32)


def pick(face, sel_ref, flux_ref, packed_ref):
    at = 0
    for d, whole in PACKED:
        size = face if whole else face // 8
        rows = dot(sel_ref[d, :size, :], flux_ref[d * face : (d + 1) * face, :])
        packed_ref[at : at + size, :] = rows.astype(bf16)
        at += size


def load_kernel(face, chunk, ahead, u_hbm, k_hbm, s_hbm, nodes_hbm, flux_ref, packed_ref, mixed, sel_ref, selt_ref, k_ref, s_ref, u_ref, nodes_ref, sems, small_sems):
    small = [
        pltpu.make_async_copy(nodes_hbm, nodes_ref, small_sems.at[0]),
        pltpu.make_async_copy(u_hbm, u_ref, small_sems.at[1]),
    ]
    for copy in small:
        copy.start()
    parts, copies = [], []
    for which, (source, target) in enumerate(((k_hbm, k_ref), (s_hbm, s_ref))):
        for i in range(target.shape[0] // chunk):
            rows = pl.ds(i * chunk, chunk)
            parts.append((which, rows))
            copies.append(pltpu.make_async_copy(source.at[rows], target.at[rows], sems.at[which, i]))
    for copy in copies[:ahead]:
        copy.start()
    for copy in small:
        copy.wait()
    slot = lax.broadcasted_iota(jnp.int32, (face, face), 0)
    u = u_ref[...]
    for i, (which, rows) in enumerate(parts):
        for d in range(8 * i // len(parts), 8 * (i + 1) // len(parts)):
            chosen = (slot == nodes_ref[d : d + 1, :] - d * face).astype(f32)
            selt_ref[d] = chosen.astype(bf16)
            sel_ref[d] = chosen.T.astype(bf16)
        copies[i].wait()
        if i + ahead < len(parts):
            copies[i + ahead].start()
        if which == 0:
            mixed[rows, :] = (0.5 * u_ref[rows, :].astype(f32) + dot(k_ref[rows, :], u)).astype(bf16)
        else:
            flux_ref[rows, :] = dot(s_ref[rows, :], mixed[...]).astype(bf16)
    pick(face, sel_ref, flux_ref, packed_ref)


def load_products(trace, kernel, inverse, nodes):
    count, width = trace.shape
    face = nodes.shape[1]
    chunk = 256 if count % 256 == 0 and 8 * face % 256 == 0 else face
    return pl.pallas_call(
        functools.partial(load_kernel, face, chunk, 4),
        out_shape=[
            shape_of((8 * face, width), bf16),
            shape_of((4 * (face + face // 8), width), bf16),
            shape_of((count, width), bf16),
            shape_of((8, face, face), bf16),
            shape_of((8, face, face), bf16),
            pltpu.VMEM((count, count), bf16),
            pltpu.VMEM((8 * face, count), bf16),
        ],
        in_specs=[hbm] * 4,
        out_specs=[vmem] * 7,
        scratch_shapes=[
            pltpu.VMEM((count, width), bf16),
            pltpu.VMEM(nodes.shape, jnp.int32),
            pltpu.SemaphoreType.DMA((2, count // chunk)),
            pltpu.SemaphoreType.DMA((2,)),
        ],
        compiler_params=params,
        cost_estimate=pl.CostEstimate(
            flops=4 * count * count * 2 * LANES, bytes_accessed=4 * count * count, transcendentals=0
        ),
        name="load_products",
    )(trace, kernel, inverse, nodes)


def load_rest_kernel(mixed_ref, s_hbm, flux_ref, s_ref, sem):
    rest = s_ref.shape[0]
    copy = pltpu.make_async_copy(s_hbm.at[pl.ds(s_hbm.shape[0] - rest, rest)], s_ref, sem)
    copy.start()
    copy.wait()
    flux_ref[...] = dot(s_ref[...], mixed_ref[...]).astype(bf16)


def load_rest(mixed, inverse, rest):
    count, width = mixed.shape
    return pl.pallas_call(
        load_rest_kernel,
        out_shape=[shape_of((rest, width), bf16), pltpu.VMEM((rest, count), bf16)],
        in_specs=[vmem, hbm],
        out_specs=[vmem] * 2,
        scratch_shapes=[pltpu.SemaphoreType.DMA],
        compiler_params=params,
        cost_estimate=pl.CostEstimate(
            flops=2 * rest * count * LANES, bytes_accessed=2 * rest * count, transcendentals=0
        ),
        name="load_rest",
    )(mixed, inverse)


def prepare_kernel(mode_ref, weight_ref, basis_ref, tall_ref):
    modes = basis_ref.shape[0]
    mode = lax.broadcasted_iota(jnp.int32, (modes, LANES), 0)
    for i in range(tall_ref.shape[0] // LANES):
        rows = pl.ds(i * LANES, LANES)
        part = jnp.where(mode == mode_ref[:, rows], weight_ref[:, rows].astype(f32), 0.0)
        basis_ref[:, rows] = part.astype(bf16)
        tall_ref[rows, :] = jnp.concatenate([part] * (LANES // modes)).T.astype(bf16)


def prepare(mode, weight):
    count = mode.shape[1]
    return pl.pallas_call(
        prepare_kernel,
        out_shape=[shape_of((MODES, count), bf16), shape_of((count, LANES), bf16)],
        in_specs=[vmem] * 2,
        out_specs=[vmem] * 2,
        compiler_params=params,
        name="prepare",
    )(mode, weight)


def products_kernel(face, chunk, state_ref, res_ref, k_ref, top_ref, rest_ref, sel_ref, tall_ref, c_ref, u_ref, flux_ref, packed_ref, entering, mixed):
    count, width = u_ref.shape
    for i in range(count // chunk):
        rows = pl.ds(i * chunk, chunk)
        following = state_ref[rows, :].astype(f32) + 0.25 * res_ref[rows, :].astype(f32)
        if c_ref is not None:
            following += dot(tall_ref[rows, : c_ref.shape[0]], c_ref[...])
        u_ref[rows, :] = following.astype(bf16)
        entering[rows, :width] = following.astype(bf16)
        if c_ref is None:
            entering[rows, width:] = tall_ref[rows, :]
    u = entering[...]
    for i in range(count // chunk):
        rows = pl.ds(i * chunk, chunk)
        mixed[rows, :] = (0.5 * entering[rows, :].astype(f32) + dot(k_ref[rows, :], u)).astype(bf16)
    m = mixed[...]
    top = top_ref.shape[0]
    for i in range(0, top, chunk):
        flux_ref[i : i + chunk, :] = dot(top_ref[i : i + chunk, :], m).astype(bf16)
    for i in range(0, count - top, chunk):
        flux_ref[top + i : top + i + chunk, :] = dot(rest_ref[i : i + chunk, :], m).astype(bf16)
    pick(face, sel_ref, flux_ref, packed_ref)


def products(state, residual, kernel, inverse, selector, tall, own):
    count, width = state.shape
    face = selector.shape[1]
    chunk = 256 if count % 256 == 0 and 8 * face % 256 == 0 else face
    wide = width + LANES if own is None else width
    operands = [state, residual, kernel, *inverse, selector, tall]
    body = functools.partial(products_kernel, face, chunk)
    if own is None:
        inner = body
        body = lambda *refs: inner(*refs[:7], None, *refs[7:])
    else:
        operands.append(own)
    return pl.pallas_call(
        body,
        out_shape=[
            shape_of((count, width), bf16),
            shape_of((count, wide), bf16),
            shape_of((4 * (face + face // 8), wide), bf16),
        ],
        in_specs=[vmem] * len(operands),
        out_specs=[vmem] * 3,
        scratch_shapes=[pltpu.VMEM((count, wide), bf16), pltpu.VMEM((count, wide), bf16)],
        compiler_params=params,
        cost_estimate=pl.CostEstimate(
            flops=4 * count * count * 2 * LANES, bytes_accessed=4 * count * count, transcendentals=0
        ),
        name="products",
    )(*operands)


def arrivals(face):
    corner = face // 8
    found = {4: (0, 0), 3: (1, 0), 6: (2, 0), 1: (3, 0)}
    found |= {7: (2, face), 5: (2, face + corner), 2: (3, face), 0: (3, face + corner)}
    return [found[d] + (face if d in (1, 3, 4, 6) else corner,) for d in range(8)]


def couple_kernel(modes, selt_ref, w_ref, wrows_ref, out_ref):
    face = selt_ref.shape[1]
    lane = lax.broadcasted_iota(jnp.int32, (face, LANES), 1)
    for d, (group, at, size) in enumerate(arrivals(face)):
        theirs = dot(selt_ref[d, :, :size], wrows_ref[group, at : at + size, :])
        mine = w_ref[d * face : (d + 1) * face, :].astype(f32)
        out_ref[d, :, :face] = selt_ref[d]
        out_ref[d, :, face:] = jnp.where(lane < modes, theirs, mine).astype(bf16)


def couple(selector_t, wide, wide_rows):
    face = selector_t.shape[1]
    return pl.pallas_call(
        functools.partial(couple_kernel, MODES),
        out_shape=shape_of((8, face, face + LANES), bf16),
        in_specs=[vmem] * 3,
        out_specs=vmem,
        compiler_params=params,
        name="couple",
    )(selector_t, wide, wide_rows)


def first_update_kernel(rows_ref, flux_ref, rest_ref, load_ref, selt_ref, basis_ref, res_ref, rhs_ref):
    face = selt_ref.shape[1]
    for d, (group, at, size) in enumerate(arrivals(face)):
        band = slice(d * face, (d + 1) * face)
        placed = dot(selt_ref[d, :, :size], rows_ref[group, at : at + size, :])
        assembled = flux_ref[band, :].astype(f32) + placed
        res_ref[band, :] = (load_ref[band, :].astype(f32) - assembled).astype(bf16)
    rest = slice(8 * face, None)
    res_ref[rest, :] = (load_ref[rest, :].astype(f32) - rest_ref[...].astype(f32)).astype(bf16)
    rhs_ref[...] = dot(basis_ref[...], res_ref[...]).astype(bf16)


def update_kernel(half, row_ref, col_ref, rows_ref, flux_ref, load_ref, couple_ref, basis_ref, c_ref, w_ref, res_ref, rhs_ref, own_ref, right):
    face = couple_ref.shape[1]
    modes = basis_ref.shape[0]
    odd, col = row_ref[0] % 2, col_ref[0]
    base = col // half * (half - 1)

    def results(row_step, col_step):
        source = (0, 1 + odd, 2 - odd)[row_step]
        beside = jnp.clip(col + col_step, base, base + half) - base
        return c_ref[source, pl.ds(pl.multiple_of(beside * modes, modes), modes), :]

    own = results(0, 0)
    own_ref[...] = own
    for d, (group, at, size) in enumerate(arrivals(face)):
        band = slice(d * face, (d + 1) * face)
        right[d, :size, :] = rows_ref[group, at : at + size, :]
        if size < face:
            right[d, size:face, :] = jnp.zeros((face - size, right.shape[2]), bf16)
        right[d, face : face + modes, :] = results(*DIRECTIONS[d])
        right[d, face + modes :, :] = own
        assembled = flux_ref[band, :].astype(f32) + dot(couple_ref[d], right[d])
        res_ref[band, :] = (load_ref[band, :].astype(f32) - assembled).astype(bf16)
    rest = slice(8 * face, None)
    assembled = flux_ref[rest, :].astype(f32) + dot(w_ref[rest, :modes], own)
    res_ref[rest, :] = (load_ref[rest, :].astype(f32) - assembled).astype(bf16)
    rhs = dot(basis_ref[...], res_ref[...]).astype(bf16)
    for i in range(rhs_ref.shape[0] // modes):
        rhs_ref[i * modes : (i + 1) * modes, :] = rhs


def settle_kernel(chunk, state_ref, res_ref, tall_ref, own_ref, out_hbm, before_ref, sem):
    copy = pltpu.make_async_copy(res_ref, out_hbm, sem)
    copy.start()
    for i in range(state_ref.shape[0] // chunk):
        rows = pl.ds(i * chunk, chunk)
        product = dot(tall_ref[rows, : own_ref.shape[0]], own_ref[...])
        gained = state_ref[rows, :].astype(f32) + 0.25 * res_ref[rows, :].astype(f32)
        before_ref[rows, :] = gained + product
    copy.wait()


def settle(state, residual, tall, own):
    count = state.shape[0]
    return pl.pallas_call(
        functools.partial(settle_kernel, 256 if count % 256 == 0 else count),
        out_shape=[shape_of(state.shape, bf16), shape_of(state.shape, f32)],
        in_specs=[vmem] * 4,
        out_specs=[hbm, vmem],
        scratch_shapes=[pltpu.SemaphoreType.DMA],
        compiler_params=params,
        name="settle",
    )(state, residual, tall, own)


def finish_kernel(chunk, before_ref, tall_ref, own_ref, trace_hbm, trace, sems):
    copies = []
    for i in range(before_ref.shape[0] // chunk):
        rows = pl.ds(i * chunk, chunk)
        product = dot(tall_ref[rows, : own_ref.shape[0]], own_ref[...])
        trace[rows, :] = (before_ref[rows, :] + product).astype(bf16)
        copies.append(pltpu.make_async_copy(trace.at[rows], trace_hbm.at[rows], sems.at[i]))
        copies[-1].start()
    for copy in copies:
        copy.wait()


def finish(before, tall, own):
    count = before.shape[0]
    chunk = 256 if count % 256 == 0 else count
    return pl.pallas_call(
        functools.partial(finish_kernel, chunk),
        out_shape=shape_of(before.shape, bf16),
        in_specs=[vmem] * 3,
        out_specs=hbm,
        scratch_shapes=[
            pltpu.VMEM(before.shape, bf16),
            pltpu.SemaphoreType.DMA((count // chunk,)),
        ],
        compiler_params=params,
        name="finish",
    )(before, tall, own)


def update(place, half, rows, flux, load, selector_t, basis, coarse, wide, coupling, copies=1):
    count, width = load.shape
    modes = basis.shape[0]
    face = selector_t.shape[1]
    outs = [shape_of((count, width), bf16), shape_of((copies * modes, width), bf16)]
    if coarse is None:
        operands = [rows, *flux, load, selector_t, basis]
        return pl.pallas_call(
            first_update_kernel,
            out_shape=outs,
            in_specs=[vmem] * 6,
            out_specs=[vmem] * 2,
            compiler_params=params,
            name="first_update",
        )(*operands)
    operands = [*place, rows, flux, load, coupling, basis, coarse, wide]
    return pl.pallas_call(
        functools.partial(update_kernel, half),
        out_shape=outs + [shape_of((modes, width), bf16)],
        in_specs=[smem] * 2 + [vmem] * 7,
        out_specs=[vmem] * 3,
        scratch_shapes=[pltpu.VMEM((8, face + LANES, width), bf16)],
        compiler_params=params,
        name="update",
    )(*operands)


def coarse_kernel(modes, half, order, row_ref, col_ref, pieces_ref, *refs):
    matrices, (mine_ref, sent_ref, full, whole) = refs[:-4], refs[-4:]
    for m in range(pieces_ref.shape[0]):
        block = row_ref[0] ^ order[m] if order else m
        full[pl.ds(pl.multiple_of(block * modes, modes), modes), :] = pieces_ref[m]
    count = mine_ref.shape[1]
    upper = col_ref[0] // half
    mine = pl.multiple_of(upper * (2 * half * modes - count), modes)
    sent = pl.multiple_of((1 - upper) * (2 * half * modes - count), modes)
    for i, matrix in enumerate(matrices):
        whole[i] = dot(matrix[...], full[...])
        mine_ref[i] = whole[i, pl.ds(mine, count), :]
        sent_ref[i] = whole[i, pl.ds(sent, count), :].astype(bf16)


def coarse_product(place, half, pieces, matrices, count, order=None):
    many, modes, width = pieces.shape
    rows, depth = matrices[0].shape
    return pl.pallas_call(
        functools.partial(coarse_kernel, modes, half, order),
        out_shape=[
            shape_of((len(matrices), count, width), f32),
            shape_of((len(matrices), count, width), bf16),
        ],
        in_specs=[smem] * 2 + [vmem] * (1 + len(matrices)),
        out_specs=[vmem] * 2,
        scratch_shapes=[
            pltpu.VMEM((depth, width), bf16),
            pltpu.VMEM((len(matrices), rows, width), f32),
        ],
        compiler_params=params,
        cost_estimate=pl.CostEstimate(
            flops=2 * len(matrices) * rows * depth * width,
            bytes_accessed=2 * len(matrices) * rows * depth,
            transcendentals=0,
        ),
        name="coarse_product",
    )(*place, pieces, *matrices)


def swap(value, axis, mask):
    return lax.ppermute(value, axis, [(i, i ^ mask) for i in range(lax.axis_size(axis))])


def cross(value, axis):
    subs, cols = lax.axis_size("sub"), lax.axis_size("col")
    pairs = []
    for sub in range(subs):
        for col in range(cols):
            to = [sub, col]
            k = 0 if axis == "sub" else 1
            n = (subs, cols)[k]
            near = to[k] + 1 if to[k] % 2 else to[k] - 1
            if 0 <= near < n or n <= 4:
                to[k] = near % n
            else:
                to[1 - k] ^= 1
            pairs.append((sub * cols + col, to[0] * cols + to[1]))
    return lax.ppermute(value, ("sub", "col"), pairs)


def onward(value, axis):
    n = lax.axis_size(axis)
    ring = list(range(0, n, 2)) + list(range(n - 1, 0, -2))
    return lax.ppermute(value, axis, [(ring[i - 1], ring[i]) for i in range(n)])


def trade(forward, backward, axis, even, meanwhile=None, first=()):
    near = swap(jnp.where(even, forward, backward), axis, 1)
    far = jnp.where(even, backward, forward)
    far, first = lax.optimization_barrier((far, first))
    far = cross(far, axis)
    done = None
    if meanwhile is not None:
        near, done = meanwhile(near)
        far, done = lax.optimization_barrier((far, done))
    return jnp.where(even, near, far), jnp.where(even, far, near), done, first


def exchange(packed, face, even, meanwhile=None, first=()):
    corner = face // 8
    group = face + 2 * corner
    right, left, done, first = trade(
        packed[:group], packed[group : 2 * group], "col", even[1], meanwhile, first
    )
    six, one = packed[2 * group : 2 * group + face], packed[2 * group + face :]
    up = jnp.concatenate([six, right[face + corner :], left[face + corner :]])
    down = jnp.concatenate([one, right[face : face + corner], left[face : face + corner]])
    above, below, _, _ = trade(up, down, "sub", even[0])
    return jnp.stack([right, left, above, below]), done, first


def sum_over_columns(value, sent):
    bit = lax.axis_size("col") // 2
    while bit:
        value = value + swap(sent, "col", bit).astype(f32)
        sent = value.astype(bf16)
        bit //= 2
    return sent


def share_of_sum(value, sent):
    bit = lax.axis_size("col") // 2
    while True:
        value = value + swap(sent, "col", bit | 1).astype(f32)
        bit //= 2
        if not bit:
            return value.astype(bf16)
        half = value.shape[0] // 2
        upper = (lax.axis_index("col") // bit) % 2 == 1
        low, high = value[:half], value[half:]
        sent = jnp.where(upper, low, high).astype(bf16)
        value = jnp.where(upper, high, low)


def local(
    trace_start,
    neumann_load,
    double_layer,
    single_inverse,
    interface_nodes,
    node_mode,
    mode_weight,
    coarse_inverse,
):
    subs, cols = lax.axis_size("sub"), lax.axis_size("col")
    row, col = lax.axis_index("sub"), lax.axis_index("col")
    trace = trace_start[0, 0]
    load = neumann_load[0, 0]
    width = trace.shape[1]
    interface = interface_nodes[0, 0]
    face = interface.shape[1]

    half = cols // 2
    place = [jnp.reshape(index, (1,)).astype(jnp.int32) for index in (row, col)]
    even = [row % 2 == 0, col % 2 == 0]
    trace, place, even = lax.optimization_barrier((trace, place, even))

    in_hbm = lambda value: pltpu.with_memory_space_constraint(value, pltpu.HBM)
    inverse = in_hbm(single_inverse[0, 0])
    edge, packed, mixed, selector, selector_t, kernel, top = load_products(
        in_hbm(trace), in_hbm(double_layer[0, 0]), inverse, in_hbm(interface)
    )
    near = swap(coarse_inverse, "sub", 1)

    def beside(near):
        near, ready = lax.optimization_barrier((near, mixed))
        return near, load_rest(ready, inverse, trace.shape[0] - edge.shape[0])

    basis, tall = prepare(node_mode[0], mode_weight[0])
    rows, (beyond, bottom), near = exchange(packed, face, even, beside, near)
    matrices = [coarse_inverse, near, onward(near, "sub")]
    inverse, flux = (top, bottom), (edge, beyond)
    state, own, coarse, wide, coupling = trace, None, None, None, None
    for iteration in range(ITERS):
        last = iteration == ITERS - 1
        residual, rhs, *own = update(
            place, half, rows, flux, load, selector_t, basis, coarse, wide, coupling, subs if last else 1
        )
        own = own[0] if own else None
        if last:
            residual, before = settle(state, residual, tall, own)
            gathered = lax.all_to_all(rhs, "sub", 0, 0, tiled=True)
            gathered, before = lax.optimization_barrier((gathered, before))
            gathered = gathered.reshape(subs, MODES, width)
            value, sent = coarse_product(
                place, half, gathered, matrices[:1], half * MODES
            )
            final = share_of_sum(value[0], sent[0])
            break
        bits = [subs >> i for i in range(1, subs.bit_length())]
        order = [0, bits[0]]
        pieces = jnp.stack([rhs, swap(rhs, "sub", bits[0])])
        state, flux, packed = products(state, residual, kernel, inverse, selector, tall, own)
        pieces, packed, matrices = lax.optimization_barrier((pieces, packed, matrices))
        rows, _, _ = exchange(packed, face, even)
        if iteration == 0:
            wide, wide_rows = flux[:, width:], rows[:, :, width:]
            flux, rows = flux[:, :width], rows[:, :, :width]
            coupling = couple(selector_t, wide, wide_rows)
        for bit in bits[1:]:
            order += [m ^ bit for m in order]
            pieces = jnp.concatenate([pieces, swap(pieces, "sub", bit)])
        coarse = sum_over_columns(*coarse_product(place, half, pieces, matrices, (half + 1) * MODES, order))
    trace = finish(before, tall, final)
    return trace[None, None], residual[None, None]


def solution(mesh):
    placed = (
        P("sub", "col", None, None),
        P("sub", "col", None, None),
        P("sub", "col", None, None),
        P("sub", "col", None, None),
        P("sub", "col", None, None),
        P("sub", "col", None),
        P("sub", "col", None),
        P("sub", "col"),
    )
    return jax.shard_map(
        local,
        mesh=mesh,
        in_specs=placed,
        out_specs=(P("sub", "col", None, None), P("sub", "col", None, None)),
        check_vma=False,
    )
```
